128 devices in a mesh: seq: 16 (over x, y), head: 8 (over z, core).
Axes of the slice: x: 4, y: 4, z: 4, core: 2. Of those that a mesh axis runs over, the one named last changes fastest.
Arguments:
- query: bfloat16 [4096, 4096], P('seq', 'head'), may hold values from -6 to 6
- key: bfloat16 [4096, 4096], P('seq', 'head'), may hold values from -6 to 6
- value: bfloat16 [4096, 4096], P('seq', 'head'), may hold values from -6 to 6
- head_gain: float32 [4096], P('head'), may hold values from 0.1 to 1.9
- out_weight: bfloat16 [4096, 4096], P('head', 'seq'), may hold values from -0.09375 to 0.09375
- stream: bfloat16 [4096, 4096], P(('seq', 'head')), may hold values from -6 to 6
- model_gain: float32 [4096], replicated, may hold values from 0.1 to 1.9
- expert_ids: int32 [4096, 8], P(('seq', 'head')), may hold values from 0 to 127, all different within a row; in each aligned block of 32 rows (0 to 31, 32 to 63, ...) at most 3 rows name the same one
- expert_gates: float32 [4096, 8], P(('seq', 'head')), may hold values from 0.1 to 0.5
- gate_weight: bfloat16 [128, 4096, 768], P(('seq', 'head')), may hold values from -0.09375 to 0.09375
- up_weight: bfloat16 [128, 4096, 768], P(('seq', 'head')), may hold values from -0.09375 to 0.09375
- down_weight: bfloat16 [128, 768, 4096], P(('seq', 'head')), may hold values from -0.21875 to 0.21875
- weight_scales: float32 [128, 3], P(('seq', 'head')), may hold values from 0.6 to 1.6
Outputs:
- layer_out: bfloat16 [4096, 4096], P(('seq', 'head'))
The draws below stay inside these ranges and needn't reach their ends.
Inputs may be any that keep to these rules, and one draw needn't show every extreme that they name: `expert_ids`: among the 32 tokens of one device (aligned blocks of rows), no expert is named more than 3 times, a bound that some block reaches; the entries of one row differ.
All inputs are finite; a program needn't handle non-finite values.
Results may differ from the reference program's by a relative error of at most 0.013.
Values may be sent and summed in bfloat16 or wider, within the bound.
No kernel may reach another device: no remote copies, remote signals or barrier semaphores. Data moves between devices by JAX's collectives and lax.ppermute only.
A program may use at most 128 MiB of HBM per device.

```python
import math
import jax
import jax.numpy as jnp
import numpy as np
from jax import lax

D = 4096
HEADS = 32
HD = 128
FF = 768
TOPK = 8
SEQ_DEV = 256
TOK_DEV = 32
EXPERTS = 128
CAP = 3
TOKENS = 4096
N_SEQ = 16
N_HEAD = 8


def shard_levels(rng, dims, split, smallest, top_value):
    factor_of, own = 1.0, jax.random.fold_in(rng, 6)
    for axis_at, parts in split:
        heights = jnp.exp(jax.random.uniform(jax.random.fold_in(own, axis_at), (parts,), jnp.float32, smallest / len(split), top_value / len(split)))
        factor_of = factor_of * jnp.repeat(heights, dims[axis_at] // parts).reshape([-1 if axis == axis_at else 1 for axis in range(len(dims))])
    return factor_of


def shared_out(rng, own, number, rows, count, top, bound, lean):
    order = jax.random.permutation(rng, count)
    packed, usual = shares(count, rows * top, bound, lean, True), shares(count, rows * top, bound, lean, False)
    places = jnp.arange(count)

    def named(tallies, rotation):
        used = int((tallies > 0).sum())
        fixed = max(1, used // 4)
        passed = fixed + (places - fixed + rotation * (used - fixed)) % max(1, count - fixed)
        return jnp.zeros((count,), jnp.int32).at[order[jnp.where(places < fixed, places, passed)]].set(jnp.asarray(tallies, jnp.int32))

    tallies = jnp.where(number % 4 == 0, named(packed, number // 4), named(usual, number - number // 4 - 1))
    mixed = jax.random.permutation(jax.random.fold_in(own, 3), count)
    donor, receiver = mixed[0:count // 2 * 2:2], mixed[1:count // 2 * 2:2]
    margin = jnp.minimum(tallies[donor] - 1, bound - tallies[receiver]) // 2
    margin = jnp.where((donor == order[0]) | (receiver == order[0]) | (tallies[receiver] == 0), 0, jnp.maximum(margin, 0))
    passed = jax.random.randint(jax.random.fold_in(own, 4), (count // 2,), 0, 1 << 20) % (margin + 1)
    tallies = tallies.at[donor].add(-passed).at[receiver].add(passed)
    members = jnp.searchsorted(jnp.cumsum(tallies), jnp.arange(rows * top), side="right").astype(jnp.int32)
    listing = members.reshape(top, rows).T
    listing = listing[jax.random.permutation(jax.random.fold_in(own, 1), rows)]
    rotation = jax.random.randint(jax.random.fold_in(own, 2), (rows, 1), 0, top)
    return jnp.take_along_axis(listing, (jnp.arange(top)[None, :] + rotation) % top, axis=1)


def shares(count, total, most, lean, full):
    portions = [(1 << 20) // math.isqrt(standing ** lean) + 1 for standing in range(1, count + 1)]
    largest = most if full else min(most, max(-(-total // count), total * portions[0] // sum(portions)))
    least = 1 if total - largest >= count - 1 else 0
    given, spare = [largest] + [least] * (count - 1), total - largest - least * (count - 1)
    while spare > 0:
        candidates = [i for i in range(1, count) if given[i] < largest] or [i for i in range(1, count) if given[i] < most]
        mass, remaining = sum([portions[i] for i in candidates]), spare
        for i in candidates:
            more = min(most - given[i], max(1, remaining * portions[i] // mass), spare)
            given[i] = given[i] + more
            spare = spare - more
    return np.array(given)


def normal_values(key, shape, width, reach, pieces=(), kind=jnp.bfloat16):
    result = jax.random.normal(key, shape, jnp.float32) * width
    if len(pieces) > 0:
        result = shard_levels(key, shape, pieces, -0.22, 0.18) * result
    return jnp.clip(result, min=-reach, max=reach).astype(kind)


def setup_inputs(seed: int = 0) -> dict:
    key_list = jax.random.split(jax.random.key(seed), 14)
    query = normal_values(key_list[0], (TOKENS, HEADS * HD), 1.0, 6.0, ((0, 16), (1, 8)))
    key = normal_values(key_list[1], (TOKENS, HEADS * HD), 1.0, 6.0, ((0, 16), (1, 8)))
    value = normal_values(key_list[2], (TOKENS, HEADS * HD), 1.0, 6.0, ((0, 16), (1, 8)))
    head_gain = jnp.clip(1.0 + 0.18 * jax.random.normal(key_list[3], (HEADS * HD,), jnp.float32), 0.1, 1.9)
    out_weight = normal_values(key_list[4], (HEADS * HD, D), (HEADS * HD) ** -0.5, 0.09375, ((0, 8), (1, 16)))
    stream = normal_values(key_list[5], (TOKENS, D), 1.0, 6.0, ((0, 128),))
    model_gain = jnp.clip(1.0 + 0.18 * jax.random.normal(key_list[6], (D,), jnp.float32), 0.1, 1.9)
    expert_ids_keys = jax.random.split(jax.random.fold_in(key_list[7], 1), TOKENS // TOK_DEV)
    expert_ids_turns = jax.random.permutation(jax.random.fold_in(key_list[7], 3), TOKENS // TOK_DEV)
    expert_ids = jax.vmap(lambda own, number: shared_out(jax.random.fold_in(key_list[7], 2), own, number, TOK_DEV, EXPERTS, TOPK, CAP, 2))(expert_ids_keys, expert_ids_turns).reshape((TOKENS, TOPK))
    expert_gates = jnp.clip(0.1 + 0.4 * jax.random.uniform(key_list[8], (TOKENS, TOPK), jnp.float32) ** shard_levels(key_list[8], (TOKENS, TOPK), ((0, 128),), -0.2, 0.2), 0.1, 0.5)
    gate_weight = normal_values(key_list[9], (EXPERTS, D, FF), D ** -0.5, 0.09375, ((0, 128),))
    up_weight = normal_values(key_list[10], (EXPERTS, D, FF), D ** -0.5, 0.09375, ((0, 128),))
    down_weight = normal_values(key_list[11], (EXPERTS, FF, D), FF ** -0.5, 0.21875, ((0, 128),))
    weight_scales = jnp.clip(jnp.exp(math.log(1.6) - 0.98082923 * jax.random.uniform(key_list[12], (EXPERTS, 3), jnp.float32) ** shard_levels(key_list[12], (EXPERTS, 3), ((0, 128),), -0.2, 0.2)), 0.6, 1.6)
    return dict(query=query, key=key, value=value, head_gain=head_gain, out_weight=out_weight, stream=stream, model_gain=model_gain, expert_ids=expert_ids, expert_gates=expert_gates, gate_weight=gate_weight, up_weight=up_weight, down_weight=down_weight, weight_scales=weight_scales)


def to_bf16_value(array):
    return lax.optimization_barrier(array.astype(jnp.bfloat16)).astype(jnp.float32)

def reference(query, key, value, head_gain, out_weight, stream, model_gain, expert_ids, expert_gates, gate_weight, up_weight, down_weight, weight_scales):
    query_blocks = query.reshape(N_SEQ, SEQ_DEV, HEADS, HD)
    key_blocks = key.reshape(N_SEQ, SEQ_DEV, HEADS, HD)
    value_blocks = value.reshape(N_SEQ, SEQ_DEV, HEADS, HD)
    causal = jnp.tril(jnp.ones((SEQ_DEV, SEQ_DEV), dtype=bool))

    def block_step(carried, slices):
        query_rows, key_rows, value_rows = slices
        query_float = query_rows.astype(jnp.float32)
        key_float = key_rows.astype(jnp.float32)
        value_float = value_rows.astype(jnp.float32)
        scores = jnp.einsum('thd,shd->hts', query_float, key_float)
        scores = to_bf16_value(jnp.where(causal[None, :, :], scores, 0.0))
        local_part = jnp.einsum('hts,shd->thd', scores, value_float)
        prior_state = to_bf16_value(carried)
        earlier_part = jnp.einsum('thd,hde->the', query_float, prior_state)
        updated = carried + jnp.einsum('shd,she->hde', key_float, value_float)
        return (updated, local_part + earlier_part)
    initial = jnp.zeros((HEADS, HD, HD), jnp.float32)
    final_state, mixed_heads = lax.scan(block_step, initial, (query_blocks, key_blocks, value_blocks))
    mixed_heads = mixed_heads.reshape(TOKENS, HEADS, HD)
    mean_square = lax.optimization_barrier(jnp.mean(mixed_heads * mixed_heads, axis=-1, keepdims=True))
    head_normed = (mixed_heads * lax.rsqrt(mean_square + 1e-06) * head_gain.reshape(HEADS, HD)).astype(jnp.bfloat16)
    head_normed = head_normed.reshape(TOKENS, HEADS * HD)
    attention = jnp.dot(head_normed.astype(jnp.float32), out_weight.astype(jnp.float32))
    residual = (stream.astype(jnp.float32) + attention).astype(jnp.bfloat16)
    residual_float = residual.astype(jnp.float32)
    mean_square = lax.optimization_barrier(jnp.mean(residual_float * residual_float, axis=-1, keepdims=True))
    normed = (residual_float * lax.rsqrt(mean_square + 1e-06) * model_gain).astype(jnp.bfloat16)
    most_rows = CAP * N_SEQ * N_HEAD

    def expert_step(expert_mix, slices):
        expert, gate_matrix, up_matrix, down_matrix, scale_row = slices
        chosen = expert_ids == expert
        token_weight = lax.optimization_barrier(jnp.sum(jnp.where(chosen, expert_gates, 0.0), axis=1))
        has_expert = jnp.any(chosen, axis=1)
        row_index = jnp.nonzero(has_expert, size=most_rows, fill_value=0)[0].astype(jnp.int32)
        live_count = jnp.sum(has_expert.astype(jnp.int32))
        is_live = (jnp.arange(most_rows, dtype=jnp.int32) < live_count).astype(jnp.float32)
        inputs = normed[row_index].astype(jnp.float32)
        gate_part = jnp.dot(inputs, gate_matrix.astype(jnp.float32)) * scale_row[0]
        up_part = jnp.dot(inputs, up_matrix.astype(jnp.float32)) * scale_row[1]
        act = to_bf16_value(jax.nn.silu(gate_part) * up_part)
        expert_rows = to_bf16_value(jnp.dot(act, down_matrix.astype(jnp.float32)) * scale_row[2])
        weighted = expert_rows * (token_weight[row_index] * is_live)[:, None]
        return (expert_mix.at[row_index].add(weighted), None)
    expert_list = jnp.arange(EXPERTS, dtype=jnp.int32)
    expert_mix, unused = lax.scan(expert_step, jnp.zeros((TOKENS, D), jnp.float32), (expert_list, gate_weight, up_weight, down_weight, weight_scales))
    return (residual_float + expert_mix).astype(jnp.bfloat16)
```

```python
import jax
import jax.numpy as jnp
from jax import lax
from jax.sharding import PartitionSpec as P

D = 4096
HD = 128
TOPK = 8
CAP = 3
NX, NY, NZ, NC = 4, 4, 4, 2
BF = jnp.bfloat16
F32 = jnp.float32


def shift_x(a, d):
    pairs = [(x * NY + y, (x + d) % NX * NY + y) for x in range(NX) for y in range(NY)]
    return lax.ppermute(a, "seq", pairs)


def shift_y(a, d):
    pairs = [(x * NY + y, x * NY + (y + d) % NY) for x in range(NX) for y in range(NY)]
    return lax.ppermute(a, "seq", pairs)


def shift_z(a, d):
    pairs = [(z * NC + c, (z + d) % NZ * NC + c) for z in range(NZ) for c in range(NC)]
    return lax.ppermute(a, "head", pairs)


def swap_core(a):
    pairs = [(z * NC + c, z * NC + 1 - c) for z in range(NZ) for c in range(NC)]
    return lax.ppermute(a, "head", pairs)


def earlier_states(block_state, x, y):
    own = block_state.astype(BF)
    total = block_state
    before = jnp.zeros_like(block_state)
    for d in range(1, NY):
        got = shift_y(own, d).astype(F32)
        total = total + got
        before = before + jnp.where(y >= d, got, 0.0)
    total = total.astype(BF)
    for d in range(1, NX):
        before = before + jnp.where(x >= d, shift_x(total, d).astype(F32), 0.0)
    return before


def sum_heads(partial, z, c):
    rows = partial.reshape(NZ, NC, -1, partial.shape[-1])
    first = c == 0
    keep = jnp.where(first, rows[:, 0], rows[:, 1])
    give = jnp.where(first, rows[:, 1], rows[:, 0]).astype(BF)
    pair = keep + swap_core(give).astype(F32)
    total = lax.dynamic_index_in_dim(pair, z, 0, False)
    low = pair.astype(BF)
    for d in range(1, NZ):
        total = total + shift_z(lax.dynamic_index_in_dim(low, (z + d) % NZ, 0, False), d).astype(F32)
    return total


def body(
    query,
    key,
    value,
    head_gain,
    out_weight,
    stream,
    model_gain,
    expert_ids,
    expert_gates,
    gate_weight,
    up_weight,
    down_weight,
    weight_scales,
):
    seq = lax.axis_index("seq")
    head = lax.axis_index("head")
    x, y, z, c = seq // NY, seq % NY, head // NC, head % NC
    seq_rows = query.shape[0]
    tok_rows = stream.shape[0]
    heads_local = head_gain.shape[0] // HD
    experts = lax.axis_size("seq") * lax.axis_size("head")
    slots = experts * CAP

    full_out = lax.all_gather(out_weight, "seq", axis=1, tiled=True)

    query_rows = query.reshape(seq_rows, heads_local, HD)
    key_rows = key.reshape(seq_rows, heads_local, HD)
    value_rows = value.reshape(seq_rows, heads_local, HD)
    block_state = jnp.einsum("shd,she->hde", key_rows, value_rows, preferred_element_type=F32)
    prior_state = earlier_states(block_state, x, y)
    scores = jnp.einsum("thd,shd->hts", query_rows, key_rows, preferred_element_type=F32)
    causal = jnp.tril(jnp.ones((seq_rows, seq_rows), dtype=bool))
    scores = jnp.where(causal[None, :, :], scores, 0.0).astype(BF)
    local_part = jnp.einsum("hts,shd->thd", scores, value_rows, preferred_element_type=F32)
    earlier_part = jnp.einsum(
        "thd,hde->the", query_rows, prior_state.astype(BF), preferred_element_type=F32
    )
    mixed_heads = local_part + earlier_part
    mean_square = jnp.mean(mixed_heads * mixed_heads, axis=-1, keepdims=True)
    head_normed = (
        mixed_heads * lax.rsqrt(mean_square + 1e-06) * head_gain.reshape(heads_local, HD)
    ).astype(BF)
    head_normed = head_normed.reshape(seq_rows, heads_local * HD)

    flat_ids = expert_ids.reshape(-1)
    n = flat_ids.shape[0]
    at = jnp.arange(n, dtype=jnp.int32)
    same = (flat_ids[:, None] == flat_ids[None, :]) & (at[None, :] < at[:, None])
    slot_index = jnp.sum(same.astype(jnp.int32), axis=1)
    target = (flat_ids * CAP + slot_index).reshape(tok_rows, TOPK)
    chosen = target[:, :, None] == jnp.arange(slots, dtype=jnp.int32)[None, None, :]
    place = jnp.any(chosen, axis=1).astype(BF)
    gates = jnp.sum(jnp.where(chosen, expert_gates[:, :, None], 0.0), axis=1)
    gates_high = gates.astype(BF)
    gates_low = (gates - gates_high.astype(F32)).astype(BF)
    gates_two = jnp.concatenate([gates_high, gates_low], axis=0)

    partial = jnp.dot(head_normed, full_out, preferred_element_type=F32)
    attention = sum_heads(partial, z, c)
    residual_float = (stream.astype(F32) + attention).astype(BF).astype(F32)
    mean_square = jnp.mean(residual_float * residual_float, axis=-1, keepdims=True)
    normed = (residual_float * lax.rsqrt(mean_square + 1e-06) * model_gain).astype(BF)

    outgoing = jnp.einsum("ts,td->sd", place, normed, preferred_element_type=F32).astype(BF)
    lanes = 128
    message = outgoing.reshape(experts, CAP * D // lanes, lanes)
    arrived = lax.all_to_all(message, ("seq", "head"), split_axis=0, concat_axis=0, tiled=True)
    slot_rows = arrived.reshape(slots, D)
    scale_row = weight_scales[0]
    gate_part = jnp.dot(slot_rows, gate_weight[0], preferred_element_type=F32) * scale_row[0]
    up_part = jnp.dot(slot_rows, up_weight[0], preferred_element_type=F32) * scale_row[1]
    act = (jax.nn.silu(gate_part) * up_part).astype(BF)
    produced = jnp.dot(act, down_weight[0], preferred_element_type=F32) * scale_row[2]
    message = produced.astype(BF).reshape(experts, CAP * D // lanes, lanes)
    results = lax.all_to_all(message, ("seq", "head"), split_axis=0, concat_axis=0, tiled=True)
    results = results.reshape(slots, D)
    both = jnp.dot(gates_two, results, preferred_element_type=F32)
    expert_mix = both[:tok_rows] + both[tok_rows:]
    return (residual_float + expert_mix).astype(BF)


def solution(mesh):
    token = P(("seq", "head"), None)
    expert = P(("seq", "head"), None, None)
    return jax.shard_map(
        body,
        mesh=mesh,
        in_specs=(
            P("seq", "head"),
            P("seq", "head"),
            P("seq", "head"),
            P("head"),
            P("head", "seq"),
            token,
            P(),
            token,
            token,
            expert,
            expert,
            expert,
            token,
        ),
        out_specs=token,
        check_vma=False,
    )
```

```python
import jax
import jax.numpy as jnp
from jax import lax
from jax.experimental import pallas as pl
from jax.experimental.pallas import tpu as pltpu
from jax.sharding import PartitionSpec as P

D = 4096
HD = 128
TOPK = 8
CAP = 3
NZ, NC = 4, 2
BF = jnp.bfloat16
F32 = jnp.float32


def shift_z(a, d):
    pairs = [(z * NC + c, (z + d) % NZ * NC + c) for z in range(NZ) for c in range(NC)]
    return lax.ppermute(a, "head", pairs)


def swap_core(a):
    pairs = [(z * NC + c, z * NC + 1 - c) for z in range(NZ) for c in range(NC)]
    return lax.ppermute(a, "head", pairs)


def earlier_states(block_state, seq):
    blocks = lax.axis_size("seq")
    parts = block_state.reshape(blocks, -1, HD)
    got = lax.all_to_all(parts, "seq", split_axis=0, concat_axis=0, tiled=True)
    sums = [jnp.zeros_like(got[0])]
    for block in range(blocks - 1):
        sums.append(sums[-1] + got[block])
    back = lax.all_to_all(jnp.stack(sums).astype(BF), "seq", split_axis=0, concat_axis=0, tiled=True)
    return back.reshape(block_state.shape)


def sum_heads(partial, z, c):
    rows = partial.reshape(NZ, NC, -1, partial.shape[-1])
    first = c == 0
    keep = jnp.where(first, rows[:, 0], rows[:, 1])
    give = jnp.where(first, rows[:, 1], rows[:, 0]).astype(BF)
    pair = keep + swap_core(give).astype(F32)
    total = lax.dynamic_index_in_dim(pair, z, 0, False)
    low = pair.astype(BF)
    for d in range(1, NZ):
        total = total + shift_z(lax.dynamic_index_in_dim(low, (z + d) % NZ, 0, False), d).astype(F32)
    return total


WIDE = 256
OUT = 1024


def expert_kernel(scale, rows, gate, up, down, out, act):
    step = pl.program_id(0)
    wide = act.shape[0]

    @pl.when(step < wide)
    def _():
        x = rows[...]
        gate_part = jnp.dot(x, gate[...], preferred_element_type=F32) * scale[0, 0]
        up_part = jnp.dot(x, up[...], preferred_element_type=F32) * scale[0, 1]
        act[step] = (gate_part / (1.0 + jnp.exp(-gate_part)) * up_part).astype(BF)

    @pl.when(step >= wide)
    def _():
        total = jnp.dot(act[0], down[0:WIDE], preferred_element_type=F32)
        for j in range(1, wide):
            total += jnp.dot(act[j], down[j * WIDE : (j + 1) * WIDE], preferred_element_type=F32)
        out[...] = (total * scale[0, 2]).astype(BF)


def run_expert(scale, rows, gate, up, down):
    count, depth = rows.shape
    hidden = gate.shape[1]
    wide = hidden // WIDE
    return pl.pallas_call(
        expert_kernel,
        out_shape=jax.ShapeDtypeStruct((count, depth), BF),
        grid=(wide + depth // OUT,),
        in_specs=[
            pl.BlockSpec(memory_space=pltpu.SMEM),
            pl.BlockSpec((count, depth), lambda i: (0, 0)),
            pl.BlockSpec((depth, WIDE), lambda i: (0, jnp.minimum(i, wide - 1))),
            pl.BlockSpec((depth, WIDE), lambda i: (0, jnp.minimum(i, wide - 1))),
            pl.BlockSpec((hidden, OUT), lambda i: (0, jnp.maximum(i - wide, 0))),
        ],
        out_specs=pl.BlockSpec((count, OUT), lambda i: (0, jnp.maximum(i - wide, 0))),
        scratch_shapes=[pltpu.VMEM((wide, count, WIDE), BF)],
        compiler_params=pltpu.CompilerParams(vmem_limit_bytes=40 << 20),
        cost_estimate=pl.CostEstimate(
            flops=6 * count * depth * hidden, bytes_accessed=6 * depth * hidden, transcendentals=count * hidden
        ),
    )(scale, rows, gate, up, down)


def body(
    query,
    key,
    value,
    head_gain,
    out_weight,
    stream,
    model_gain,
    expert_ids,
    expert_gates,
    gate_weight,
    up_weight,
    down_weight,
    weight_scales,
):
    seq = lax.axis_index("seq")
    head = lax.axis_index("head")
    z, c = head // NC, head % NC
    seq_rows = query.shape[0]
    tok_rows = stream.shape[0]
    heads_local = head_gain.shape[0] // HD
    experts = lax.axis_size("seq") * lax.axis_size("head")
    slots = experts * CAP

    full_out = lax.all_gather(out_weight, "seq", axis=1, tiled=True)

    query_rows = query.reshape(seq_rows, heads_local, HD)
    key_rows = key.reshape(seq_rows, heads_local, HD)
    value_rows = value.reshape(seq_rows, heads_local, HD)
    block_state = jnp.einsum("shd,she->hde", key_rows, value_rows, preferred_element_type=F32)
    prior_state = earlier_states(block_state, seq)
    scores = jnp.einsum("thd,shd->hts", query_rows, key_rows, preferred_element_type=F32)
    causal = jnp.tril(jnp.ones((seq_rows, seq_rows), dtype=bool))
    scores = jnp.where(causal[None, :, :], scores, 0.0).astype(BF)
    local_part = jnp.einsum("hts,shd->thd", scores, value_rows, preferred_element_type=F32)
    earlier_part = jnp.einsum(
        "thd,hde->the", query_rows, prior_state, preferred_element_type=F32
    )
    mixed_heads = local_part + earlier_part
    mean_square = jnp.mean(mixed_heads * mixed_heads, axis=-1, keepdims=True)
    head_normed = (
        mixed_heads * lax.rsqrt(mean_square + 1e-06) * head_gain.reshape(heads_local, HD)
    ).astype(BF)
    head_normed = head_normed.reshape(seq_rows, heads_local * HD)

    flat_ids = expert_ids.reshape(-1)
    n = flat_ids.shape[0]
    at = jnp.arange(n, dtype=jnp.int32)
    same = (flat_ids[:, None] == flat_ids[None, :]) & (at[None, :] < at[:, None])
    slot_index = jnp.sum(same.astype(jnp.int32), axis=1)
    target = (flat_ids * CAP + slot_index).reshape(tok_rows, TOPK)
    chosen = target[:, :, None] == jnp.arange(slots, dtype=jnp.int32)[None, None, :]
    place = jnp.any(chosen, axis=1).astype(BF)
    gates = jnp.sum(jnp.where(chosen, expert_gates[:, :, None], 0.0), axis=1)
    gates_high = gates.astype(BF)
    gates_low = (gates - gates_high.astype(F32)).astype(BF)
    gates_two = jnp.concatenate([gates_high, gates_low], axis=0)

    partial = jnp.dot(head_normed, full_out, preferred_element_type=F32)
    attention = sum_heads(partial, z, c)
    residual_float = (stream.astype(F32) + attention).astype(BF).astype(F32)
    mean_square = jnp.mean(residual_float * residual_float, axis=-1, keepdims=True)
    normed = (residual_float * lax.rsqrt(mean_square + 1e-06) * model_gain).astype(BF)

    outgoing = jnp.einsum("ts,td->sd", place, normed, preferred_element_type=F32).astype(BF)
    lanes = 128
    message = outgoing.reshape(experts, CAP * D // lanes, lanes)
    arrived = lax.all_to_all(message, ("seq", "head"), split_axis=0, concat_axis=0, tiled=True)
    slot_rows = arrived.reshape(slots, D)
    produced = run_expert(weight_scales, slot_rows, gate_weight[0], up_weight[0], down_weight[0])
    message = produced.reshape(experts, CAP * D // lanes, lanes)
    results = lax.all_to_all(message, ("seq", "head"), split_axis=0, concat_axis=0, tiled=True)
    results = results.reshape(slots, D)
    both = jnp.dot(gates_two, results, preferred_element_type=F32)
    expert_mix = both[:tok_rows] + both[tok_rows:]
    return (residual_float + expert_mix).astype(BF)


def solution(mesh):
    token = P(("seq", "head"), None)
    expert = P(("seq", "head"), None, None)
    return jax.shard_map(
        body,
        mesh=mesh,
        in_specs=(
            P("seq", "head"),
            P("seq", "head"),
            P("seq", "head"),
            P("head"),
            P("head", "seq"),
            token,
            P(),
            token,
            token,
            expert,
            expert,
            expert,
            token,
        ),
        out_specs=token,
        check_vma=False,
    )
```

```python
import functools

import jax
import jax.numpy as jnp
from jax import lax
from jax.experimental import pallas as pl
from jax.experimental.pallas import tpu as pltpu
from jax.sharding import PartitionSpec as P

D = 4096
HD = 128
TOPK = 8
CAP = 3
NX, NY, NZ, NC = 4, 4, 4, 2
LANES = 128
HALF = D // 2
BLOCKS = HALF // LANES
WIDE = 256
BF = jnp.bfloat16
F32 = jnp.float32


def from_x(a, d):
    pairs = [((x + d) % NX * NY + y, x * NY + y) for x in range(NX) for y in range(NY)]
    return lax.ppermute(a, "seq", pairs)


def from_y(a, d):
    pairs = [(x * NY + (y + d) % NY, x * NY + y) for x in range(NX) for y in range(NY)]
    return lax.ppermute(a, "seq", pairs)


def to_z(a, d):
    pairs = [(z * NC + c, (z + d) % NZ * NC + c) for z in range(NZ) for c in range(NC)]
    return lax.ppermute(a, "head", pairs)


def swap_core(a):
    pairs = [(z * NC + c, z * NC + 1 - c) for z in range(NZ) for c in range(NC)]
    return lax.ppermute(a, "head", pairs)


def earlier_states(block_state):
    blocks = lax.axis_size("seq")
    parts = block_state.reshape(blocks, -1, HD)
    got = lax.all_to_all(parts, "seq", split_axis=0, concat_axis=0, tiled=True)
    at = jnp.arange(blocks)
    earlier = (at[None, :] < at[:, None])[:, :, None, None]
    sums = jnp.sum(jnp.where(earlier, got[None], 0.0), axis=1).astype(BF)
    back = lax.all_to_all(sums, "seq", split_axis=0, concat_axis=0, tiled=True)
    return back.reshape(block_state.shape)


def gather_weight(weight):
    first, second = weight[:, :LANES], weight[:, LANES:]
    line_y = [first] + [from_y(first, d) for d in range(1, NY)]
    line_x = [second] + [from_x(second, d) for d in range(1, NX)]
    line_y = jnp.concatenate(line_y, axis=1)
    line_x = jnp.concatenate(line_x, axis=1)
    first = [line_y] + [from_x(line_y, d) for d in range(1, NX)]
    second = [line_x] + [from_y(line_x, d) for d in range(1, NY)]
    return first, second


def sum_pair(partial, c):
    rows = partial.reshape(NZ, NC, -1, partial.shape[-1])
    first = c == 0
    keep = jnp.where(first, rows[:, 0], rows[:, 1])
    give = jnp.where(first, rows[:, 1], rows[:, 0]).astype(BF)
    return keep + swap_core(give).astype(F32)


def spread_z(pair, z):
    own = lax.dynamic_index_in_dim(pair, z, 0, False)
    low = pair.astype(BF)
    return own, [to_z(lax.dynamic_index_in_dim(low, (z + d) % NZ, 0, False), d) for d in range(1, NZ)]


def place_kernel(half, pos, target, own, one, two, three, stream, res, message):
    tok = own.shape[0]
    x, y = pos[0], pos[1]
    for j in range(BLOCKS):
        lanes = slice(j * LANES, (j + 1) * LANES)
        if half == 0:
            block = (x + j // NY) % NX * NY + (y + j % NY) % NY
        else:
            block = (x + j % NX) % NX * NY + (y + j // NX) % NY
        at = pl.multiple_of(block * 2 * LANES + half * LANES, LANES)
        total = (
            own[:, lanes]
            + one[:, lanes].astype(F32)
            + two[:, lanes].astype(F32)
            + three[:, lanes].astype(F32)
            + stream[:, pl.ds(at, LANES)].astype(F32)
        )
        res[:, pl.ds(block, 1), :] = total.astype(BF).astype(F32)[:, None, :]
    message[...] = jnp.zeros_like(message)

    def one_token(t, carry):
        row = res[t].astype(BF)
        for k in range(TOPK):
            message[target[t, k]] = row
        return carry

    lax.fori_loop(0, tok, one_token, 0)


def place(half, pos, target, own, parts, stream, slots):
    tok = own.shape[0]
    smem = pl.BlockSpec(memory_space=pltpu.SMEM)
    vmem = pl.BlockSpec(memory_space=pltpu.VMEM)
    return pl.pallas_call(
        functools.partial(place_kernel, half),
        out_shape=(
            jax.ShapeDtypeStruct((tok, BLOCKS, LANES), F32),
            jax.ShapeDtypeStruct((slots, BLOCKS, LANES), BF),
        ),
        in_specs=[smem, smem] + [vmem] * 5,
        out_specs=(vmem, vmem),
        compiler_params=pltpu.CompilerParams(vmem_limit_bytes=16 << 20),
        cost_estimate=pl.CostEstimate(flops=1 << 20, bytes_accessed=3 << 20, transcendentals=0),
    )(pos, target, own, *parts, stream)


def first_kernel(rows, gain, gate, up, gate_out, up_out, squares, scaled):
    @pl.when(pl.program_id(0) == 0)
    def _():
        x = rows[...].astype(F32)
        squares[...] = jnp.broadcast_to(jnp.sum(x * x, axis=1, keepdims=True), squares.shape)
        scaled[...] = (x * gain[...]).astype(BF)

    x = scaled[...]
    gate_out[...] = jnp.dot(x, gate[...].reshape(HALF, WIDE), preferred_element_type=F32)
    up_out[...] = jnp.dot(x, up[...].reshape(HALF, WIDE), preferred_element_type=F32)


def second_kernel(scale, rows, gain, gate, up, gate_in, up_in, squares, act, scaled, factor):
    @pl.when(pl.program_id(0) == 0)
    def _():
        x = rows[...].astype(F32)
        total = squares[...] + jnp.sum(x * x, axis=1, keepdims=True)
        factor[...] = lax.rsqrt(total * (1.0 / D) + 1e-06)
        scaled[...] = (x * gain[...]).astype(BF)

    x = scaled[...]
    by_row = factor[:, :1]
    gate_part = jnp.dot(x, gate[...].reshape(HALF, WIDE), preferred_element_type=F32) + gate_in[...]
    up_part = jnp.dot(x, up[...].reshape(HALF, WIDE), preferred_element_type=F32) + up_in[...]
    gate_part = gate_part * (by_row * scale[0, 0])
    up_part = up_part * (by_row * scale[0, 1])
    act[...] = (gate_part / (1.0 + jnp.exp(-gate_part)) * up_part).astype(BF)


def hidden_half(half, rows, gain, gate, up, rest=None):
    count, hidden = rows.shape[0], gate.shape[1]
    gate = gate.reshape(BLOCKS, 2, LANES, hidden)
    up = up.reshape(BLOCKS, 2, LANES, hidden)
    weight = pl.BlockSpec((BLOCKS, None, LANES, WIDE), lambda i: (0, half, 0, i))
    part = pl.BlockSpec((count, WIDE), lambda i: (0, i))
    row = pl.BlockSpec((count, HALF), lambda i: (0, 0))
    one = pl.BlockSpec((1, HALF), lambda i: (0, 0))
    narrow = pl.BlockSpec((count, LANES), lambda i: (0, 0))
    scratch = [pltpu.VMEM((count, HALF), BF)]
    common = dict(
        grid=(hidden // WIDE,),
        compiler_params=pltpu.CompilerParams(vmem_limit_bytes=24 << 20),
        cost_estimate=pl.CostEstimate(
            flops=4 * count * HALF * hidden, bytes_accessed=4 * HALF * hidden, transcendentals=0
        ),
    )
    if rest is None:
        sums = jax.ShapeDtypeStruct((count, hidden), F32)
        return pl.pallas_call(
            first_kernel,
            out_shape=(sums, sums, jax.ShapeDtypeStruct((count, LANES), F32)),
            in_specs=[row, one, weight, weight],
            out_specs=(part, part, narrow),
            scratch_shapes=scratch,
            **common,
        )(rows, gain, gate, up)
    scale, gate_in, up_in, squares = rest
    return pl.pallas_call(
        second_kernel,
        out_shape=jax.ShapeDtypeStruct((count, hidden), BF),
        in_specs=[pl.BlockSpec(memory_space=pltpu.SMEM), row, one, weight, weight, part, part, narrow],
        out_specs=part,
        scratch_shapes=scratch + [pltpu.VMEM((count, LANES), F32)],
        **common,
    )(scale, rows, gain, gate, up, gate_in, up_in, squares)


def down_kernel(scale, act, one, two, three, four, out):
    weight = jnp.concatenate([one[...], two[...], three[...], four[...]], axis=1)
    total = jnp.dot(act[...], weight, preferred_element_type=F32)
    out[...] = (total * scale[0, 2]).astype(BF)


def down_half(half, scale, act, down):
    count, hidden = act.shape
    group = 4

    def columns(g):
        return pl.BlockSpec((hidden, LANES), lambda i: (0, 2 * (group * i + g) + half))

    return pl.pallas_call(
        down_kernel,
        out_shape=jax.ShapeDtypeStruct((count, HALF), BF),
        grid=(BLOCKS // group,),
        in_specs=[pl.BlockSpec(memory_space=pltpu.SMEM), pl.BlockSpec((count, hidden), lambda i: (0, 0))]
        + [columns(g) for g in range(group)],
        out_specs=pl.BlockSpec((count, group * LANES), lambda i: (0, i)),
        compiler_params=pltpu.CompilerParams(vmem_limit_bytes=16 << 20),
        cost_estimate=pl.CostEstimate(
            flops=2 * count * HALF * hidden, bytes_accessed=2 * HALF * hidden, transcendentals=0
        ),
    )(scale, act, down, down, down, down)


def mix_kernel(last, target, gates, results, res, *rest):
    tok = res.shape[0]
    mixed = rest[-1]

    def one_token(t, carry):
        total = res[t]
        add = gates[t, 0] * results[target[t, 0]].astype(F32)
        for k in range(1, TOPK):
            add += gates[t, k] * results[target[t, k]].astype(F32)
        mixed[t] = total + add
        return carry

    lax.fori_loop(0, tok, one_token, 0)
    if last:
        first, out = rest[0], rest[1]
        for block in range(BLOCKS):
            at = block * 2 * LANES
            out[:, at : at + LANES] = first[:, block, :].astype(BF)
            out[:, at + LANES : at + 2 * LANES] = mixed[:, block, :].astype(BF)


def mix(target, gates, results, res, first=None):
    tok = res.shape[0]
    smem = pl.BlockSpec(memory_space=pltpu.SMEM)
    vmem = pl.BlockSpec(memory_space=pltpu.VMEM)
    last = first is not None
    shape = jax.ShapeDtypeStruct((tok, D), BF) if last else jax.ShapeDtypeStruct(res.shape, F32)
    return pl.pallas_call(
        functools.partial(mix_kernel, last),
        out_shape=shape,
        in_specs=[smem, smem, vmem, vmem] + [vmem] * last,
        out_specs=vmem,
        scratch_shapes=[pltpu.VMEM(res.shape, F32)] * last,
        compiler_params=pltpu.CompilerParams(vmem_limit_bytes=16 << 20),
        cost_estimate=pl.CostEstimate(flops=1 << 20, bytes_accessed=3 << 20, transcendentals=0),
    )(target, gates, results, res, *([first] if last else []))


def body(
    query,
    key,
    value,
    head_gain,
    out_weight,
    stream,
    model_gain,
    expert_ids,
    expert_gates,
    gate_weight,
    up_weight,
    down_weight,
    weight_scales,
):
    seq = lax.axis_index("seq")
    head = lax.axis_index("head")
    x, y, z, c = seq // NY, seq % NY, head // NC, head % NC
    pos = jnp.stack([x, y]).astype(jnp.int32)
    seq_rows = query.shape[0]
    tok_rows = stream.shape[0]
    heads_local = head_gain.shape[0] // HD
    experts = lax.axis_size("seq") * lax.axis_size("head")
    slots = experts * CAP

    pieces = gather_weight(out_weight)

    query_rows = query.reshape(seq_rows, heads_local, HD)
    key_rows = key.reshape(seq_rows, heads_local, HD)
    value_rows = value.reshape(seq_rows, heads_local, HD)
    block_state = jnp.einsum("shd,she->hde", key_rows, value_rows, preferred_element_type=F32)
    prior_state = earlier_states(block_state)
    scores = jnp.einsum("thd,shd->hts", query_rows, key_rows, preferred_element_type=F32)
    causal = jnp.tril(jnp.ones((seq_rows, seq_rows), dtype=bool))
    scores = jnp.where(causal[None, :, :], scores, 0.0).astype(BF)
    local_part = jnp.einsum("hts,shd->thd", scores, value_rows, preferred_element_type=F32)
    earlier_part = jnp.einsum("thd,hde->the", query_rows, prior_state, preferred_element_type=F32)
    mixed_heads = local_part + earlier_part
    mean_square = jnp.mean(mixed_heads * mixed_heads, axis=-1, keepdims=True)
    head_normed = (
        mixed_heads * lax.rsqrt(mean_square + 1e-06) * head_gain.reshape(heads_local, HD)
    ).astype(BF)
    head_normed = head_normed.reshape(seq_rows, heads_local * HD)

    flat_ids = expert_ids.reshape(-1)
    at = jnp.arange(flat_ids.shape[0], dtype=jnp.int32)
    same = (flat_ids[:, None] == flat_ids[None, :]) & (at[None, :] < at[:, None])
    slot_index = jnp.sum(same.astype(jnp.int32), axis=1)
    target = (flat_ids * CAP + slot_index).reshape(tok_rows, TOPK)
    gains = model_gain.reshape(BLOCKS, 2, LANES)

    def exchange(rows):
        message = rows.reshape(experts, CAP * BLOCKS, LANES)
        got = lax.all_to_all(message, ("seq", "head"), split_axis=0, concat_axis=0, tiled=True)
        return got.reshape(slots, BLOCKS, LANES)

    residual, arrived = [], []
    source = head_normed
    for half in range(2):
        partial = jnp.concatenate(
            [jnp.dot(source, piece, preferred_element_type=F32) for piece in pieces[half]], axis=1
        )
        pair = sum_pair(partial, c)
        if half == 0:
            source, pair = lax.optimization_barrier((source, pair))
        own, parts = spread_z(pair, z)
        res, message = place(half, pos, target, own, parts, stream, slots)
        residual.append(res)
        arrived.append(exchange(message).reshape(slots, HALF))

    rest = None
    for half in range(2):
        gain = gains[:, half].reshape(1, HALF)
        rest = hidden_half(half, arrived[half], gain, gate_weight[0], up_weight[0], rest)
        if half == 0:
            rest = (weight_scales, *rest)
    act = rest
    first = None
    for half in range(2):
        produced = down_half(half, weight_scales, act, down_weight[0])
        results = exchange(produced.reshape(slots, BLOCKS, LANES))
        first = mix(target, expert_gates, results, residual[half], first)
    return first


def solution(mesh):
    token = P(("seq", "head"), None)
    expert = P(("seq", "head"), None, None)
    return jax.shard_map(
        body,
        mesh=mesh,
        in_specs=(
            P("seq", "head"),
            P("seq", "head"),
            P("seq", "head"),
            P("head"),
            P("head", "seq"),
            token,
            P(),
            token,
            token,
            expert,
            expert,
            expert,
            token,
        ),
        out_specs=token,
        check_vma=False,
    )
```

```python
import jax
import jax.numpy as jnp
from jax import lax
from jax.experimental import pallas as pl
from jax.experimental.pallas import tpu as pltpu
from jax.sharding import PartitionSpec as P

D = 4096
HD = 128
TOPK = 8
CAP = 3
NX, NY, NZ, NC = 4, 4, 4, 2
LANES = 128
BLOCKS = D // LANES
WIDE = 256
OUT = 1024
BF = jnp.bfloat16
F32 = jnp.float32


SMEM = pl.BlockSpec(memory_space=pltpu.SMEM)
VMEM = pl.BlockSpec(memory_space=pltpu.VMEM)


def params(mib):
    return pltpu.CompilerParams(vmem_limit_bytes=mib << 20)


def cost(flops, size):
    return pl.CostEstimate(flops=flops, bytes_accessed=size, transcendentals=0)


def to_x(a, d):
    pairs = [(x * NY + y, (x + d) % NX * NY + y) for x in range(NX) for y in range(NY)]
    return lax.ppermute(a, "seq", pairs)


def to_y(a, d):
    pairs = [(x * NY + y, x * NY + (y + d) % NY) for x in range(NX) for y in range(NY)]
    return lax.ppermute(a, "seq", pairs)


def to_z(a, d):
    pairs = [(z * NC + c, (z + d) % NZ * NC + c) for z in range(NZ) for c in range(NC)]
    return lax.ppermute(a, "head", pairs)


def swap_core(a):
    pairs = [(z * NC + c, z * NC + 1 - c) for z in range(NZ) for c in range(NC)]
    return lax.ppermute(a, "head", pairs)


def mixed_kernel(pos, query, before, one, two, three, local, gain, out):
    heads = before.shape[0]
    masks = [jnp.where(pos[0] >= d, 1.0, 0.0) for d in (1, 2, 3)]
    for h in range(heads):
        lanes = slice(h * HD, (h + 1) * HD)
        prior = before[h]
        for mask, got in zip(masks, (one, two, three)):
            prior += mask * got[h].astype(F32)
        mixed = local[:, lanes] + jnp.dot(query[:, lanes], prior.astype(BF), preferred_element_type=F32)
        mean_square = jnp.mean(mixed * mixed, axis=-1, keepdims=True)
        out[:, lanes] = (mixed * lax.rsqrt(mean_square + 1e-06) * gain[:, lanes]).astype(BF)


def mixed_heads(pos, query, before, totals, local, gain):
    return pl.pallas_call(
        mixed_kernel,
        out_shape=jax.ShapeDtypeStruct(query.shape, BF),
        in_specs=[SMEM] + [VMEM] * 7,
        out_specs=VMEM,
        compiler_params=params(16),
        cost_estimate=cost(1 << 25, 2 << 20),
    )(pos, query, before, *totals, local, gain)


def project_kernel(pos, *refs):
    tokens, weights, (keep, give, rows) = refs[:NX], refs[NX : NX + NY], refs[NX + NY :]
    tok, wide = keep.shape[1], weights[0].shape[1]
    mine = pl.multiple_of(pos[3] * tok, tok)
    other = pl.multiple_of(tok - pos[3] * tok, tok)
    for dx in range(NX):
        for dy in range(NY):
            rows[:, dy * wide : (dy + 1) * wide] = jnp.dot(
                tokens[dx][...], weights[dy][...], preferred_element_type=F32
            )
        for z in range(NZ):
            keep[dx * NZ + z] = rows[pl.ds(z * NC * tok + mine, tok), :]
            give[dx * NZ + z] = rows[pl.ds(z * NC * tok + other, tok), :].astype(BF)


def project(pos, tokens, weights, tok):
    wide = NY * weights[0].shape[1]
    shape = (NX * NZ, tok, wide)
    count, depth = tokens[0].shape
    return pl.pallas_call(
        project_kernel,
        out_shape=(jax.ShapeDtypeStruct(shape, F32), jax.ShapeDtypeStruct(shape, BF)),
        in_specs=[SMEM] + [VMEM] * (NX + NY),
        out_specs=(VMEM, VMEM),
        scratch_shapes=[pltpu.VMEM((count, wide), F32)],
        compiler_params=params(24),
        cost_estimate=cost(2 * NX * count * depth * wide, 5 << 20),
    )(pos, *tokens, *weights)


def pair_kernel(pos, keep, got, own, one, two, three):
    z = pos[2]
    for dx in range(NX):
        at = dx * NZ + z
        own[dx] = keep[at] + got[at].astype(F32)
        for d, out in ((1, one), (2, two), (3, three)):
            at = dx * NZ + lax.rem(z + d, NZ)
            out[dx] = (keep[at] + got[at].astype(F32)).astype(BF)


def pair_sums(pos, keep, got):
    shape = (NX, *keep.shape[1:])
    low = jax.ShapeDtypeStruct(shape, BF)
    return pl.pallas_call(
        pair_kernel,
        out_shape=(jax.ShapeDtypeStruct(shape, F32), low, low, low),
        in_specs=[SMEM, VMEM, VMEM],
        out_specs=(VMEM,) * 4,
        compiler_params=params(16),
        cost_estimate=cost(1 << 20, 5 << 20),
    )(pos, keep, got)


def place_kernel(pos, target, own, one, two, three, stream, gain, res, message, total, scaled):
    tok = own.shape[0]
    wide = 2 * LANES
    x, y = pos[0], pos[1]
    squares = jnp.zeros((tok, LANES), F32)
    places = []
    for dx, part in enumerate((own, one, two, three)):
        for dy in range(NY):
            seq = lax.rem(x + NX - dx, NX) * NY + lax.rem(y + dy, NY)
            at = pl.multiple_of(seq * wide, wide)
            value = part[:, dy * wide : (dy + 1) * wide].astype(F32) + stream[:, pl.ds(at, wide)].astype(F32)
            value = value.astype(BF).astype(F32)
            j = dx * NY + dy
            total[:, j * wide : (j + 1) * wide] = value
            for half in range(2):
                cut = value[:, half * LANES : (half + 1) * LANES]
                squares += cut * cut
                res[:, pl.ds(seq * 2 + half, 1), :] = cut[:, None, :]
            places.append((j, seq, at))
    factor = lax.rsqrt(jnp.sum(squares, axis=1, keepdims=True) * (1.0 / D) + 1e-06)
    for j, seq, at in places:
        value = total[:, j * wide : (j + 1) * wide] * factor * gain[:, pl.ds(at, wide)]
        for half in range(2):
            scaled[:, pl.ds(seq * 2 + half, 1), :] = value[:, half * LANES : (half + 1) * LANES][:, None, :]
    message[...] = jnp.zeros_like(message)

    def one_token(t, carry):
        row = scaled[t].astype(BF)
        for k in range(TOPK):
            message[target[t, k]] = row
        return carry

    lax.fori_loop(0, tok, one_token, 0)


def place(pos, target, parts, stream, gain, slots):
    tok = stream.shape[0]
    return pl.pallas_call(
        place_kernel,
        out_shape=(
            jax.ShapeDtypeStruct((tok, BLOCKS, LANES), F32),
            jax.ShapeDtypeStruct((slots, BLOCKS, LANES), BF),
        ),
        in_specs=[SMEM, SMEM] + [VMEM] * 6,
        out_specs=(VMEM, VMEM),
        scratch_shapes=[pltpu.VMEM((tok, D), F32), pltpu.VMEM((tok, BLOCKS, LANES), F32)],
        compiler_params=params(24),
        cost_estimate=cost(1 << 20, 5 << 20),
    )(pos, target, *parts, stream, gain)


def expert_kernel(scale, rows, gate, up, down, out, act):
    step = pl.program_id(0)
    wide = act.shape[0]

    @pl.when(step < wide)
    def _():
        x = rows[...]
        gate_part = jnp.dot(x, gate[...], preferred_element_type=F32) * scale[0, 0]
        up_part = jnp.dot(x, up[...], preferred_element_type=F32) * scale[0, 1]
        act[step] = (gate_part / (1.0 + jnp.exp(-gate_part)) * up_part).astype(BF)

    @pl.when(step >= wide)
    def _():
        total = jnp.dot(act[0], down[0:WIDE], preferred_element_type=F32)
        for j in range(1, wide):
            total += jnp.dot(act[j], down[j * WIDE : (j + 1) * WIDE], preferred_element_type=F32)
        out[...] = (total * scale[0, 2]).astype(BF)


def run_expert(scale, rows, gate, up, down):
    count, depth = rows.shape
    hidden = gate.shape[1]
    wide = hidden // WIDE
    return pl.pallas_call(
        expert_kernel,
        out_shape=jax.ShapeDtypeStruct((count, depth), BF),
        grid=(wide + depth // OUT,),
        in_specs=[
            pl.BlockSpec(memory_space=pltpu.SMEM),
            pl.BlockSpec((count, depth), lambda i: (0, 0)),
            pl.BlockSpec((depth, WIDE), lambda i: (0, jnp.minimum(i, wide - 1))),
            pl.BlockSpec((depth, WIDE), lambda i: (0, jnp.minimum(i, wide - 1))),
            pl.BlockSpec((hidden, OUT), lambda i: (0, jnp.maximum(i - wide, 0))),
        ],
        out_specs=pl.BlockSpec((count, OUT), lambda i: (0, jnp.maximum(i - wide, 0))),
        scratch_shapes=[pltpu.VMEM((wide, count, WIDE), BF)],
        compiler_params=pltpu.CompilerParams(vmem_limit_bytes=60 << 20),
        cost_estimate=pl.CostEstimate(
            flops=6 * count * depth * hidden, bytes_accessed=6 * depth * hidden, transcendentals=count * hidden
        ),
    )(scale, rows, gate, up, down)


def mix_kernel(target, gates, results, res, out, mixed):
    tok = res.shape[0]

    def one_token(t, carry):
        add = gates[t, 0] * results[target[t, 0]].astype(F32)
        for k in range(1, TOPK):
            add += gates[t, k] * results[target[t, k]].astype(F32)
        mixed[t] = res[t] + add
        return carry

    lax.fori_loop(0, tok, one_token, 0)
    for block in range(BLOCKS):
        out[:, block * LANES : (block + 1) * LANES] = mixed[:, block, :].astype(BF)


def mix(target, gates, results, res):
    tok = res.shape[0]
    return pl.pallas_call(
        mix_kernel,
        out_shape=jax.ShapeDtypeStruct((tok, D), BF),
        in_specs=[SMEM, SMEM, VMEM, VMEM],
        out_specs=VMEM,
        scratch_shapes=[pltpu.VMEM(res.shape, F32)],
        compiler_params=params(16),
        cost_estimate=cost(1 << 20, 4 << 20),
    )(target, gates, results, res)


def body(
    query,
    key,
    value,
    head_gain,
    out_weight,
    stream,
    model_gain,
    expert_ids,
    expert_gates,
    gate_weight,
    up_weight,
    down_weight,
    weight_scales,
):
    seq = lax.axis_index("seq")
    head = lax.axis_index("head")
    x, y, z, c = seq // NY, seq % NY, head // NC, head % NC
    pos = jnp.stack([x, y, z, c]).astype(jnp.int32)
    seq_rows = query.shape[0]
    tok_rows = stream.shape[0]
    heads_local = head_gain.shape[0] // HD
    experts = lax.axis_size("seq") * lax.axis_size("head")
    slots = experts * CAP

    query_rows = query.reshape(seq_rows, heads_local, HD)
    key_rows = key.reshape(seq_rows, heads_local, HD)
    value_rows = value.reshape(seq_rows, heads_local, HD)
    block_state = jnp.einsum("shd,she->hde", key_rows, value_rows, preferred_element_type=F32)
    low = block_state.astype(BF)
    line, before = block_state, jnp.zeros_like(block_state)
    for d in range(1, NY):
        got = to_y(low, d).astype(F32)
        line = line + got
        before = before + jnp.where(y >= d, got, 0.0)
    low = line.astype(BF)
    totals = [to_x(low, d) for d in range(1, NX)]
    weights = [out_weight] + [to_y(out_weight, NY - d) for d in range(1, NY)]

    scores = jnp.einsum("thd,shd->hts", query_rows, key_rows, preferred_element_type=F32)
    causal = jnp.tril(jnp.ones((seq_rows, seq_rows), dtype=bool))
    scores = jnp.where(causal[None, :, :], scores, 0.0).astype(BF)
    local_part = jnp.einsum("hts,shd->thd", scores, value_rows, preferred_element_type=F32)
    local_part = local_part.reshape(seq_rows, heads_local * HD)
    head_normed = mixed_heads(pos, query, before, totals, local_part, head_gain[None])

    flat_ids = expert_ids.reshape(-1)
    at = jnp.arange(flat_ids.shape[0], dtype=jnp.int32)
    same = (flat_ids[:, None] == flat_ids[None, :]) & (at[None, :] < at[:, None])
    slot_index = jnp.sum(same.astype(jnp.int32), axis=1)
    target = (flat_ids * CAP + slot_index).reshape(tok_rows, TOPK)

    def exchange(rows):
        message = rows.reshape(experts, CAP * BLOCKS, LANES)
        got = lax.all_to_all(message, ("seq", "head"), split_axis=0, concat_axis=0, tiled=True)
        return got.reshape(slots, BLOCKS, LANES)

    tokens = [head_normed] + [to_x(head_normed, NX - d) for d in range(1, NX)]
    keep, give = project(pos, tokens, weights, tok_rows)
    own, *low = pair_sums(pos, keep, swap_core(give))
    for d in range(1, NZ):
        own = own + to_z(low[d - 1], d).astype(F32)
    parts = [own[0]] + [to_x(own[d].astype(BF), d) for d in range(1, NX)]
    res, message = place(pos, target, parts, stream, model_gain[None], slots)
    slot_rows = exchange(message).reshape(slots, D)
    produced = run_expert(weight_scales, slot_rows, gate_weight[0], up_weight[0], down_weight[0])
    results = exchange(produced.reshape(slots, BLOCKS, LANES))
    return mix(target, expert_gates, results, res)


def solution(mesh):
    token = P(("seq", "head"), None)
    expert = P(("seq", "head"), None, None)
    return jax.shard_map(
        body,
        mesh=mesh,
        in_specs=(
            P("seq", "head"),
            P("seq", "head"),
            P("seq", "head"),
            P("head"),
            P("head", "seq"),
            token,
            P(),
            token,
            token,
            expert,
            expert,
            expert,
            token,
        ),
        out_specs=token,
        check_vma=False,
    )
```

```python
import jax
import jax.numpy as jnp
from jax import lax
from jax.experimental import pallas as pl
from jax.experimental.pallas import tpu as pltpu
from jax.sharding import PartitionSpec as P

D = 4096
HD = 128
TOPK = 8
CAP = 3
AXES = ("x", "y", "z", "c")
NX, NY, NZ, NC = 4, 4, 4, 2
LANES = 128
BLOCKS = D // LANES
DEEP = 512
OUT = 1024
BF = jnp.bfloat16
F32 = jnp.float32


SMEM = pl.BlockSpec(memory_space=pltpu.SMEM)
VMEM = pl.BlockSpec(memory_space=pltpu.VMEM)


def params(mib):
    return pltpu.CompilerParams(vmem_limit_bytes=mib << 20)


def cost(flops, size):
    return pl.CostEstimate(flops=flops, bytes_accessed=size, transcendentals=0)


def shift(a, axis, d):
    n = lax.axis_size(axis)
    return lax.ppermute(a, axis, [(i, (i + d) % n) for i in range(n)])


def gather_line(a, axis):
    n = lax.axis_size(axis)
    return [a] + [shift(a, axis, n - d) for d in range(1, n)]


def mixed_kernel(pos, query, before, one, two, three, local, gain, out):
    heads = before.shape[0]
    masks = [jnp.where(pos[0] >= d, 1.0, 0.0) for d in (1, 2, 3)]
    for h in range(heads):
        lanes = slice(h * HD, (h + 1) * HD)
        prior = before[h]
        for mask, got in zip(masks, (one, two, three)):
            prior += mask * got[h].astype(F32)
        mixed = local[:, lanes] + jnp.dot(query[:, lanes], prior.astype(BF), preferred_element_type=F32)
        mean_square = jnp.mean(mixed * mixed, axis=-1, keepdims=True)
        out[:, lanes] = (mixed * lax.rsqrt(mean_square + 1e-06) * gain[:, lanes]).astype(BF)


def mixed_heads(pos, query, before, totals, local, gain):
    return pl.pallas_call(
        mixed_kernel,
        out_shape=jax.ShapeDtypeStruct(query.shape, BF),
        in_specs=[SMEM] + [VMEM] * 7,
        out_specs=VMEM,
        compiler_params=params(16),
        cost_estimate=cost(1 << 25, 2 << 20),
    )(pos, query, before, *totals, local, gain)


def project_kernel(pos, *refs):
    tokens, weights, (keep, give, rows) = refs[:NX], refs[NX : NX + NY], refs[NX + NY :]
    tok, wide = keep.shape[1], weights[0].shape[1]
    mine = pl.multiple_of(pos[3] * tok, tok)
    other = pl.multiple_of(tok - pos[3] * tok, tok)
    for dx in range(NX):
        for dy in range(NY):
            rows[:, dy * wide : (dy + 1) * wide] = jnp.dot(
                tokens[dx][...], weights[dy][...], preferred_element_type=F32
            )
        for z in range(NZ):
            keep[dx * NZ + z] = rows[pl.ds(z * NC * tok + mine, tok), :]
            give[dx * NZ + z] = rows[pl.ds(z * NC * tok + other, tok), :].astype(BF)


def project(pos, tokens, weights, tok):
    wide = NY * weights[0].shape[1]
    shape = (NX * NZ, tok, wide)
    count, depth = tokens[0].shape
    return pl.pallas_call(
        project_kernel,
        out_shape=(jax.ShapeDtypeStruct(shape, F32), jax.ShapeDtypeStruct(shape, BF)),
        in_specs=[SMEM] + [VMEM] * (NX + NY),
        out_specs=(VMEM, VMEM),
        scratch_shapes=[pltpu.VMEM((count, wide), F32)],
        compiler_params=params(24),
        cost_estimate=cost(2 * NX * count * depth * wide, 5 << 20),
    )(pos, *tokens, *weights)


def pair_kernel(pos, keep, got, own, one, two, three):
    z = pos[2]
    for dx in range(NX):
        at = dx * NZ + z
        own[dx] = keep[at] + got[at].astype(F32)
        for d, out in ((1, one), (2, two), (3, three)):
            at = dx * NZ + lax.rem(z + d, NZ)
            out[dx] = (keep[at] + got[at].astype(F32)).astype(BF)


def pair_sums(pos, keep, got):
    shape = (NX, *keep.shape[1:])
    low = jax.ShapeDtypeStruct(shape, BF)
    return pl.pallas_call(
        pair_kernel,
        out_shape=(jax.ShapeDtypeStruct(shape, F32), low, low, low),
        in_specs=[SMEM, VMEM, VMEM],
        out_specs=(VMEM,) * 4,
        compiler_params=params(16),
        cost_estimate=cost(1 << 20, 5 << 20),
    )(pos, keep, got)


def quarter_kernel(pos, own, one, two, three, *refs):
    stream, out = refs[:NX], refs[NX]
    wide = 2 * LANES
    y = pos[1]
    for dx in range(NX):
        for dy in range(NY):
            lanes = slice(dy * wide, (dy + 1) * wide)
            at = pl.multiple_of(lax.rem(y + dy, NY) * wide, wide)
            total = (
                own[dx, :, lanes]
                + one[dx, :, lanes].astype(F32)
                + two[dx, :, lanes].astype(F32)
                + three[dx, :, lanes].astype(F32)
                + stream[dx][:, pl.ds(at, wide)].astype(F32)
            )
            out[dx, :, pl.ds(at, wide)] = total.astype(BF)


def quarter(pos, own, parts, stream):
    return pl.pallas_call(
        quarter_kernel,
        out_shape=jax.ShapeDtypeStruct(own.shape, BF),
        in_specs=[SMEM] + [VMEM] * (NZ + NX),
        out_specs=VMEM,
        compiler_params=params(16),
        cost_estimate=cost(1 << 20, 3 << 20),
    )(pos, own, *parts, *stream)


def norm_kernel(pos, *refs):
    quarters, gain, normed, res = refs[:NX], refs[NX], refs[NX + 1], refs[NX + 2]
    tok, wide = quarters[0].shape[1:]
    x = pos[0]
    at = [pl.multiple_of(lax.rem(x + d, NX) * wide, wide) for d in range(NX)]
    for b in range(NX):
        values = [quarters[d][(b - d) % NX].astype(F32) for d in range(NX)]
        squares = values[0] * values[0]
        for value in values[1:]:
            squares += value * value
        factor = lax.rsqrt(jnp.sum(squares, axis=1, keepdims=True) * (1.0 / D) + 1e-06)
        for d in range(NX):
            lanes = pl.ds(at[d], wide)
            normed[b * tok : (b + 1) * tok, lanes] = (values[d] * factor * gain[:, lanes]).astype(BF)
            if b == 0:
                res[:, lanes] = values[d].astype(BF)


def norm(pos, quarters, gain):
    tok = quarters[0].shape[1]
    return pl.pallas_call(
        norm_kernel,
        out_shape=(jax.ShapeDtypeStruct((NX * tok, D), BF), jax.ShapeDtypeStruct((tok, D), BF)),
        in_specs=[SMEM] + [VMEM] * (NX + 1),
        out_specs=(VMEM, VMEM),
        compiler_params=params(16),
        cost_estimate=cost(1 << 21, 3 << 20),
    )(pos, *quarters, gain)


def place_kernel(where, own, other, message):
    tokens = own.shape[0]
    for j in range(0, D, OUT):
        lanes = slice(j, j + OUT)
        total = jnp.dot(where[:, :tokens], own[:, lanes], preferred_element_type=F32)
        total += jnp.dot(where[:, tokens:], other[:, lanes], preferred_element_type=F32)
        message[:, lanes] = total.astype(BF)


def place(where, own, other):
    return pl.pallas_call(
        place_kernel,
        out_shape=jax.ShapeDtypeStruct((where.shape[0], D), BF),
        in_specs=[VMEM] * 3,
        out_specs=VMEM,
        compiler_params=params(16),
        cost_estimate=cost(2 * where.shape[0] * where.shape[1] * D, 5 << 20),
    )(where, own, other)


def expert_kernel(scale, rows, gate, up, down, out, x, wg, wu, wd, gates, ups, act, part, done, in_sem, down_sem, out_sem):
    depth, hidden = wg.shape
    groups = OUT // LANES
    loads, downs, stores = [], [], []
    for i, j in enumerate(range(0, depth, DEEP)):
        at = pl.ds(j, DEEP)
        for k, (source, into) in enumerate(((rows, x), (gate, wg), (up, wu))):
            view = (source.at[:, at], into.at[:, at]) if k == 0 else (source.at[at], into.at[at])
            loads.append(pltpu.make_async_copy(*view, in_sem.at[3 * i + k]))
            loads[-1].start()
    for i, j in enumerate(range(0, depth, OUT)):
        at = pl.ds(j, OUT)
        downs.append(pltpu.make_async_copy(down.at[:, at], wd.at[:, at], down_sem.at[i]))
        downs[-1].start()
    for i, j in enumerate(range(0, depth, DEEP)):
        for load in loads[3 * i : 3 * i + 3]:
            load.wait()
        cut = x[:, j : j + DEEP]
        gate_part = jnp.dot(cut, wg[j : j + DEEP], preferred_element_type=F32)
        up_part = jnp.dot(cut, wu[j : j + DEEP], preferred_element_type=F32)
        if i == 0:
            gates[...] = gate_part
            ups[...] = up_part
        else:
            gates[...] += gate_part
            ups[...] += up_part
    gate_part = gates[...] * scale[0, 0]
    act[...] = (gate_part / (1.0 + jnp.exp(-gate_part)) * (ups[...] * scale[0, 1])).astype(BF)
    for i, j in enumerate(range(0, depth, OUT)):
        downs[i].wait()
        total = jnp.dot(act[...], wd[:, j : j + OUT], preferred_element_type=F32) * scale[0, 2]
        for g in range(groups):
            part[:, g, :] = total[:, g * LANES : (g + 1) * LANES]
        at = pl.ds(i * groups, groups)
        done[:, i * groups : (i + 1) * groups, :] = part[...].astype(BF)
        stores.append(pltpu.make_async_copy(done.at[:, at, :], out.at[:, at, :], out_sem.at[i]))
        stores[-1].start()
    for store in stores:
        store.wait()


def run_expert(scale, rows, gate, up, down):
    count, depth = rows.shape
    hidden = gate.shape[1]
    anywhere = pl.BlockSpec(memory_space=pl.ANY)
    return pl.pallas_call(
        expert_kernel,
        out_shape=jax.ShapeDtypeStruct((count, BLOCKS, LANES), BF),
        in_specs=[SMEM] + [anywhere] * 4,
        out_specs=anywhere,
        scratch_shapes=[
            pltpu.VMEM((count, depth), BF),
            pltpu.VMEM((depth, hidden), BF),
            pltpu.VMEM((depth, hidden), BF),
            pltpu.VMEM((hidden, depth), BF),
            pltpu.VMEM((count, hidden), F32),
            pltpu.VMEM((count, hidden), F32),
            pltpu.VMEM((count, hidden), BF),
            pltpu.VMEM((count, OUT // LANES, LANES), F32),
            pltpu.VMEM((count, BLOCKS, LANES), BF),
            pltpu.SemaphoreType.DMA((3 * depth // DEEP,)),
            pltpu.SemaphoreType.DMA((depth // OUT,)),
            pltpu.SemaphoreType.DMA((depth // OUT,)),
        ],
        compiler_params=params(58),
        cost_estimate=cost(6 * count * depth * hidden, 6 * depth * hidden),
    )(scale, rows, gate, up, down)


def mix_kernel(target, gates, results, res, out, mixed):
    tok = res.shape[0]

    def one_token(t, carry):
        add = gates[t, 0] * results[target[t, 0]].astype(F32)
        for k in range(1, TOPK):
            add += gates[t, k] * results[target[t, k]].astype(F32)
        mixed[t] = add
        return carry

    lax.fori_loop(0, tok, one_token, 0)
    for block in range(BLOCKS):
        lanes = slice(block * LANES, (block + 1) * LANES)
        out[:, lanes] = (res[:, lanes].astype(F32) + mixed[:, block, :]).astype(BF)


def mix(target, gates, results, res):
    tok = res.shape[0]
    return pl.pallas_call(
        mix_kernel,
        out_shape=jax.ShapeDtypeStruct((tok, D), BF),
        in_specs=[SMEM, SMEM, VMEM, VMEM],
        out_specs=VMEM,
        scratch_shapes=[pltpu.VMEM((tok, BLOCKS, LANES), F32)],
        compiler_params=params(16),
        cost_estimate=cost(1 << 20, 4 << 20),
    )(target, gates, results, res)


def body(
    query,
    key,
    value,
    head_gain,
    out_weight,
    stream,
    model_gain,
    expert_ids,
    expert_gates,
    gate_weight,
    up_weight,
    down_weight,
    weight_scales,
):
    x, y, z, c = [lax.axis_index(axis) for axis in AXES]
    pos = jnp.stack([x, y, z, c]).astype(jnp.int32)
    seq_rows = query.shape[0]
    tok_rows = stream.shape[0]
    heads_local = head_gain.shape[0] // HD
    experts = NX * NY * NZ * NC
    slots = experts * CAP

    query_rows = query.reshape(seq_rows, heads_local, HD)
    key_rows = key.reshape(seq_rows, heads_local, HD)
    value_rows = value.reshape(seq_rows, heads_local, HD)
    block_state = jnp.einsum("shd,she->hde", key_rows, value_rows, preferred_element_type=F32)
    low = block_state.astype(BF)
    line, before = block_state, jnp.zeros_like(block_state)
    for d in range(1, NY):
        got = shift(low, "y", d).astype(F32)
        line = line + got
        before = before + jnp.where(y >= d, got, 0.0)
    low = line.astype(BF)
    totals = [shift(low, "x", d) for d in range(1, NX)]
    weights = gather_line(out_weight, "y")

    scores = jnp.einsum("thd,shd->hts", query_rows, key_rows, preferred_element_type=F32)
    causal = jnp.tril(jnp.ones((seq_rows, seq_rows), dtype=bool))
    scores = jnp.where(causal[None, :, :], scores, 0.0).astype(BF)
    local_part = jnp.einsum("hts,shd->thd", scores, value_rows, preferred_element_type=F32)
    local_part = local_part.reshape(seq_rows, heads_local * HD)
    head_normed = mixed_heads(pos, query, before, totals, local_part, head_gain[None])

    flat_ids = expert_ids.reshape(-1)
    at = jnp.arange(flat_ids.shape[0], dtype=jnp.int32)
    same = (flat_ids[:, None] == flat_ids[None, :]) & (at[None, :] < at[:, None])
    slot_index = jnp.sum(same.astype(jnp.int32), axis=1)
    target = (flat_ids * CAP + slot_index).reshape(tok_rows, TOPK)

    head_normed, weights = lax.optimization_barrier((head_normed, weights))
    tokens = gather_line(head_normed, "x")
    keep, give = project(pos, tokens, weights, tok_rows)
    own, *low = pair_sums(pos, keep, shift(give, "c", 1))
    parts = [shift(low[d - 1], "z", d) for d in range(1, NZ)]
    own, target, stream = lax.optimization_barrier((own, target, stream))
    line_target = jnp.concatenate(gather_line(target.T, "x"), axis=1)
    line_target = jnp.concatenate([line_target, shift(line_target, "c", 1)], axis=1)
    token = jnp.arange(NC * NX * tok_rows, dtype=jnp.int32)
    piece = token // tok_rows
    token_block = (c + piece // NX) % NC * NX + (x + piece % NX) % NX
    row = jnp.arange(slots, dtype=jnp.int32)
    plane = row // (NC * NX * CAP)
    row_block = row // CAP % (NC * NX)
    wanted = ((x * NY * NZ + plane) * NC + c) * CAP + row % CAP
    where = jnp.any(line_target[:, None, :] == wanted[None, :, None], axis=0)
    where = (where & (token_block[None, :] == row_block[:, None])).astype(BF)
    back = target // CAP
    back = (back % (NY * NZ * NC) * NX + back // (NY * NZ * NC)) * CAP + target % CAP

    wide = D // NX
    stream_parts = [
        lax.dynamic_slice_in_dim(stream, (x + NX - d) % NX * wide, wide, axis=1) for d in range(NX)
    ]
    stream_parts = stream_parts[:1] + [shift(stream_parts[d], "x", NX - d) for d in range(1, NX)]

    residual = quarter(pos, own, parts, stream_parts)
    quarters = gather_line(residual, "x")
    quarters, where, back = lax.optimization_barrier((quarters, where, back))
    normed, res = norm(pos, quarters, model_gain[None])
    message = place(where, normed, shift(normed, "c", 1))
    slot_rows = lax.all_to_all(
        message.reshape(NY * NZ, -1, D), ("y", "z"), split_axis=0, concat_axis=0, tiled=True
    ).reshape(slots, D)
    produced = run_expert(weight_scales, slot_rows, gate_weight[0], up_weight[0], down_weight[0])
    results = lax.all_to_all(
        produced.reshape(experts, CAP * BLOCKS, LANES), ("y", "z", "c", "x"), split_axis=0, concat_axis=0, tiled=True
    )
    return mix(back, expert_gates, results.reshape(slots, BLOCKS, LANES), res)


def solution(mesh):
    chips = jax.sharding.Mesh(mesh.devices.reshape(NX, NY, NZ, NC), AXES)
    seq, head = AXES[:2], AXES[2:]
    token = P(AXES, None)
    expert = P(AXES, None, None)
    return jax.shard_map(
        body,
        mesh=chips,
        in_specs=(
            P(seq, head),
            P(seq, head),
            P(seq, head),
            P(head),
            P(head, seq),
            token,
            P(),
            token,
            token,
            expert,
            expert,
            expert,
            token,
        ),
        out_specs=token,
        check_vma=False,
    )
```

```python
import jax
import jax.numpy as jnp
from jax import lax
from jax.experimental import pallas as pl
from jax.experimental.pallas import tpu as pltpu
from jax.sharding import PartitionSpec as P

D = 4096
HD = 128
TOPK = 8
CAP = 3
AXES = ("x", "y", "z", "c")
NX, NY, NZ, NC = 4, 4, 4, 2
LANES = 128
BLOCKS = D // LANES
DEEP = 512
OUT = 1024
BF = jnp.bfloat16
F32 = jnp.float32


SMEM = pl.BlockSpec(memory_space=pltpu.SMEM)
VMEM = pl.BlockSpec(memory_space=pltpu.VMEM)


def params(mib):
    return pltpu.CompilerParams(vmem_limit_bytes=mib << 20)


def cost(flops, size):
    return pl.CostEstimate(flops=flops, bytes_accessed=size, transcendentals=0)


def shift(a, axis, d):
    n = lax.axis_size(axis)
    return lax.ppermute(a, axis, [(i, (i + d) % n) for i in range(n)])


def gather_line(a, axis):
    n = lax.axis_size(axis)
    return [a] + [shift(a, axis, n - d) for d in range(1, n)]


def mixed_kernel(pos, query, before, one, two, three, local, gain, out):
    heads = before.shape[0]
    masks = [jnp.where(pos[0] >= d, 1.0, 0.0) for d in (1, 2, 3)]
    for h in range(heads):
        lanes = slice(h * HD, (h + 1) * HD)
        prior = before[h]
        for mask, got in zip(masks, (one, two, three)):
            prior += mask * got[h].astype(F32)
        mixed = local[:, lanes] + jnp.dot(query[:, lanes], prior.astype(BF), preferred_element_type=F32)
        mean_square = jnp.mean(mixed * mixed, axis=-1, keepdims=True)
        out[:, lanes] = (mixed * lax.rsqrt(mean_square + 1e-06) * gain[:, lanes]).astype(BF)


def mixed_heads(pos, query, before, totals, local, gain):
    return pl.pallas_call(
        mixed_kernel,
        out_shape=jax.ShapeDtypeStruct(query.shape, BF),
        in_specs=[SMEM] + [VMEM] * 7,
        out_specs=VMEM,
        compiler_params=params(16),
        cost_estimate=cost(1 << 25, 2 << 20),
    )(pos, query, before, *totals, local, gain)


def project_kernel(pos, *refs):
    tokens, weights, (keep, give, rows) = refs[:NX], refs[NX : NX + NY], refs[NX + NY :]
    tok, wide = keep.shape[1], weights[0].shape[1]
    mine = pl.multiple_of(pos[3] * tok, tok)
    other = pl.multiple_of(tok - pos[3] * tok, tok)
    for dx in range(NX):
        for dy in range(NY):
            rows[:, dy * wide : (dy + 1) * wide] = jnp.dot(
                tokens[dx][...], weights[dy][...], preferred_element_type=F32
            )
        for z in range(NZ):
            keep[dx * NZ + z] = rows[pl.ds(z * NC * tok + mine, tok), :]
            give[dx * NZ + z] = rows[pl.ds(z * NC * tok + other, tok), :].astype(BF)


def project(pos, tokens, weights, tok):
    wide = NY * weights[0].shape[1]
    shape = (NX * NZ, tok, wide)
    count, depth = tokens[0].shape
    return pl.pallas_call(
        project_kernel,
        out_shape=(jax.ShapeDtypeStruct(shape, F32), jax.ShapeDtypeStruct(shape, BF)),
        in_specs=[SMEM] + [VMEM] * (NX + NY),
        out_specs=(VMEM, VMEM),
        scratch_shapes=[pltpu.VMEM((count, wide), F32)],
        compiler_params=params(24),
        cost_estimate=cost(2 * NX * count * depth * wide, 5 << 20),
    )(pos, *tokens, *weights)


def pair_kernel(pos, keep, got, own, one, two, three):
    z = pos[2]
    for dx in range(NX):
        at = dx * NZ + z
        own[dx] = keep[at] + got[at].astype(F32)
        for d, out in ((1, one), (2, two), (3, three)):
            at = dx * NZ + lax.rem(z + d, NZ)
            out[dx] = (keep[at] + got[at].astype(F32)).astype(BF)


def pair_sums(pos, keep, got):
    shape = (NX, *keep.shape[1:])
    low = jax.ShapeDtypeStruct(shape, BF)
    return pl.pallas_call(
        pair_kernel,
        out_shape=(jax.ShapeDtypeStruct(shape, F32), low, low, low),
        in_specs=[SMEM, VMEM, VMEM],
        out_specs=(VMEM,) * 4,
        compiler_params=params(16),
        cost_estimate=cost(1 << 20, 5 << 20),
    )(pos, keep, got)


def quarter_kernel(pos, own, one, two, three, *refs):
    stream, out = refs[:NX], refs[NX]
    wide = 2 * LANES
    y = pos[1]
    for dx in range(NX):
        for dy in range(NY):
            lanes = slice(dy * wide, (dy + 1) * wide)
            at = pl.multiple_of(lax.rem(y + dy, NY) * wide, wide)
            total = (
                own[dx, :, lanes]
                + one[dx, :, lanes].astype(F32)
                + two[dx, :, lanes].astype(F32)
                + three[dx, :, lanes].astype(F32)
                + stream[dx][:, pl.ds(at, wide)].astype(F32)
            )
            out[dx, :, pl.ds(at, wide)] = total.astype(BF)


def quarter(pos, own, parts, stream):
    return pl.pallas_call(
        quarter_kernel,
        out_shape=jax.ShapeDtypeStruct(own.shape, BF),
        in_specs=[SMEM] + [VMEM] * (NZ + NX),
        out_specs=VMEM,
        compiler_params=params(16),
        cost_estimate=cost(1 << 20, 3 << 20),
    )(pos, own, *parts, *stream)


def norm_kernel(pos, *refs):
    quarters, gain, normed, res = refs[:NX], refs[NX], refs[NX + 1], refs[NX + 2]
    tok, wide = quarters[0].shape[1:]
    x = pos[0]
    at = [pl.multiple_of(lax.rem(x + d, NX) * wide, wide) for d in range(NX)]
    for b in range(NX):
        values = [quarters[d][(b - d) % NX].astype(F32) for d in range(NX)]
        squares = values[0] * values[0]
        for value in values[1:]:
            squares += value * value
        factor = lax.rsqrt(jnp.sum(squares, axis=1, keepdims=True) * (1.0 / D) + 1e-06)
        for d in range(NX):
            lanes = pl.ds(at[d], wide)
            normed[b * tok : (b + 1) * tok, lanes] = (values[d] * factor * gain[:, lanes]).astype(BF)
            if b == 0:
                res[:, lanes] = values[d].astype(BF)


def norm(pos, quarters, gain):
    tok = quarters[0].shape[1]
    return pl.pallas_call(
        norm_kernel,
        out_shape=(jax.ShapeDtypeStruct((NX * tok, D), BF), jax.ShapeDtypeStruct((tok, D), BF)),
        in_specs=[SMEM] + [VMEM] * (NX + 1),
        out_specs=(VMEM, VMEM),
        compiler_params=params(16),
        cost_estimate=cost(1 << 21, 3 << 20),
    )(pos, *quarters, gain)


def place_kernel(pos, *refs):
    targets, (own, other, message, where) = refs[:NX], refs[NX:]
    x, c = pos[0], pos[3]
    tok = targets[0].shape[1]
    slots, tokens = where.shape[0], own.shape[0]
    row = lax.broadcasted_iota(jnp.int32, (slots, tok), 0)
    block = row // CAP % (NC * NX)
    wanted = ((x * NY * NZ + row // (NC * NX * CAP)) * NC + c) * CAP + row % CAP
    for core in range(NC):
        for d in range(NX):
            mine = block == lax.rem(c + core, NC) * NX + lax.rem(x + d, NX)
            found = jnp.zeros((slots, tok), jnp.bool_)
            for k in range(TOPK):
                at = core * TOPK + k
                found |= targets[d][at : at + 1, :] == wanted
            piece = core * NX + d
            where[:, piece * tok : (piece + 1) * tok] = jnp.where(mine & found, 1.0, 0.0).astype(BF)
    for j in range(0, D, OUT):
        lanes = slice(j, j + OUT)
        total = jnp.dot(where[:, :tokens], own[:, lanes], preferred_element_type=F32)
        total += jnp.dot(where[:, tokens:], other[:, lanes], preferred_element_type=F32)
        message[:, lanes] = total.astype(BF)


def place(pos, targets, own, other):
    slots = NX * NY * NZ * NC * CAP
    return pl.pallas_call(
        place_kernel,
        out_shape=jax.ShapeDtypeStruct((slots, D), BF),
        in_specs=[SMEM] + [VMEM] * (NX + 2),
        out_specs=VMEM,
        scratch_shapes=[pltpu.VMEM((slots, 2 * own.shape[0]), BF)],
        compiler_params=params(16),
        cost_estimate=cost(4 * slots * own.shape[0] * D, 5 << 20),
    )(pos, *targets, own, other)


def expert_kernel(scale, rows, gate, up, down, out, x, wg, wu, wd, gates, ups, act, part, done, in_sem, down_sem, out_sem):
    depth, hidden = wg.shape
    groups = OUT // LANES
    loads, downs, stores = [], [], []
    for i, j in enumerate(range(0, depth, DEEP)):
        at = pl.ds(j, DEEP)
        for k, (source, into) in enumerate(((rows, x), (gate, wg), (up, wu))):
            view = (source.at[:, at], into.at[:, at]) if k == 0 else (source.at[at], into.at[at])
            loads.append(pltpu.make_async_copy(*view, in_sem.at[3 * i + k]))
            loads[-1].start()
    for i, j in enumerate(range(0, depth, OUT)):
        at = pl.ds(j, OUT)
        downs.append(pltpu.make_async_copy(down.at[:, at], wd.at[:, at], down_sem.at[i]))
        downs[-1].start()
    for i, j in enumerate(range(0, depth, DEEP)):
        for load in loads[3 * i : 3 * i + 3]:
            load.wait()
        cut = x[:, j : j + DEEP]
        gate_part = jnp.dot(cut, wg[j : j + DEEP], preferred_element_type=F32)
        up_part = jnp.dot(cut, wu[j : j + DEEP], preferred_element_type=F32)
        if i == 0:
            gates[...] = gate_part
            ups[...] = up_part
        else:
            gates[...] += gate_part
            ups[...] += up_part
    gate_part = gates[...] * scale[0, 0]
    act[...] = (gate_part / (1.0 + jnp.exp(-gate_part)) * (ups[...] * scale[0, 1])).astype(BF)
    for i, j in enumerate(range(0, depth, OUT)):
        downs[i].wait()
        total = jnp.dot(act[...], wd[:, j : j + OUT], preferred_element_type=F32) * scale[0, 2]
        for g in range(groups):
            part[:, g, :] = total[:, g * LANES : (g + 1) * LANES]
        at = pl.ds(i * groups, groups)
        done[:, i * groups : (i + 1) * groups, :] = part[...].astype(BF)
        stores.append(pltpu.make_async_copy(done.at[:, at, :], out.at[:, at, :], out_sem.at[i]))
        stores[-1].start()
    for store in stores:
        store.wait()


def run_expert(scale, rows, gate, up, down):
    count, depth = rows.shape
    hidden = gate.shape[1]
    anywhere = pl.BlockSpec(memory_space=pl.ANY)
    return pl.pallas_call(
        expert_kernel,
        out_shape=jax.ShapeDtypeStruct((count, BLOCKS, LANES), BF),
        in_specs=[SMEM] + [anywhere] * 4,
        out_specs=anywhere,
        scratch_shapes=[
            pltpu.VMEM((count, depth), BF),
            pltpu.VMEM((depth, hidden), BF),
            pltpu.VMEM((depth, hidden), BF),
            pltpu.VMEM((hidden, depth), BF),
            pltpu.VMEM((count, hidden), F32),
            pltpu.VMEM((count, hidden), F32),
            pltpu.VMEM((count, hidden), BF),
            pltpu.VMEM((count, OUT // LANES, LANES), F32),
            pltpu.VMEM((count, BLOCKS, LANES), BF),
            pltpu.SemaphoreType.DMA((3 * depth // DEEP,)),
            pltpu.SemaphoreType.DMA((depth // OUT,)),
            pltpu.SemaphoreType.DMA((depth // OUT,)),
        ],
        compiler_params=params(58),
        cost_estimate=cost(6 * count * depth * hidden, 6 * depth * hidden),
    )(scale, rows, gate, up, down)


def mix_kernel(target, gates, results, res, out, mixed):
    tok = res.shape[0]

    def one_token(t, carry):
        add = gates[t, 0] * results[target[t, 0]].astype(F32)
        for k in range(1, TOPK):
            add += gates[t, k] * results[target[t, k]].astype(F32)
        mixed[t] = add
        return carry

    lax.fori_loop(0, tok, one_token, 0)
    for block in range(BLOCKS):
        lanes = slice(block * LANES, (block + 1) * LANES)
        out[:, lanes] = (res[:, lanes].astype(F32) + mixed[:, block, :]).astype(BF)


def mix(target, gates, results, res):
    tok = res.shape[0]
    return pl.pallas_call(
        mix_kernel,
        out_shape=jax.ShapeDtypeStruct((tok, D), BF),
        in_specs=[SMEM, SMEM, VMEM, VMEM],
        out_specs=VMEM,
        scratch_shapes=[pltpu.VMEM((tok, BLOCKS, LANES), F32)],
        compiler_params=params(16),
        cost_estimate=cost(1 << 20, 4 << 20),
    )(target, gates, results, res)


def body(
    query,
    key,
    value,
    head_gain,
    out_weight,
    stream,
    model_gain,
    expert_ids,
    expert_gates,
    gate_weight,
    up_weight,
    down_weight,
    weight_scales,
):
    x, y, z, c = [lax.axis_index(axis) for axis in AXES]
    pos = jnp.stack([x, y, z, c]).astype(jnp.int32)
    seq_rows = query.shape[0]
    tok_rows = stream.shape[0]
    heads_local = head_gain.shape[0] // HD
    experts = NX * NY * NZ * NC
    slots = experts * CAP

    query_rows = query.reshape(seq_rows, heads_local, HD)
    key_rows = key.reshape(seq_rows, heads_local, HD)
    value_rows = value.reshape(seq_rows, heads_local, HD)
    block_state = jnp.einsum("shd,she->hde", key_rows, value_rows, preferred_element_type=F32)
    low = block_state.astype(BF)
    line, before = block_state, jnp.zeros_like(block_state)
    for d in range(1, NY):
        got = shift(low, "y", d).astype(F32)
        line = line + got
        before = before + jnp.where(y >= d, got, 0.0)
    low = line.astype(BF)
    totals = [shift(low, "x", d) for d in range(1, NX)]
    weights = gather_line(out_weight, "y")

    scores = jnp.einsum("thd,shd->hts", query_rows, key_rows, preferred_element_type=F32)
    causal = jnp.tril(jnp.ones((seq_rows, seq_rows), dtype=bool))
    scores = jnp.where(causal[None, :, :], scores, 0.0).astype(BF)
    local_part = jnp.einsum("hts,shd->thd", scores, value_rows, preferred_element_type=F32)
    local_part = local_part.reshape(seq_rows, heads_local * HD)
    head_normed = mixed_heads(pos, query, before, totals, local_part, head_gain[None])

    flat_ids = expert_ids.reshape(-1)
    at = jnp.arange(flat_ids.shape[0], dtype=jnp.int32)
    same = (flat_ids[:, None] == flat_ids[None, :]) & (at[None, :] < at[:, None])
    slot_index = jnp.sum(same.astype(jnp.int32), axis=1)
    target = (flat_ids * CAP + slot_index).reshape(tok_rows, TOPK)

    both = jnp.concatenate([target.T, shift(target.T, "c", 1)], axis=0)
    wide = D // NX
    stream_parts = [
        lax.dynamic_slice_in_dim(stream, (x + NX - d) % NX * wide, wide, axis=1) for d in range(NX)
    ]
    back = target // CAP
    back = (back % (NY * NZ * NC) * NX + back // (NY * NZ * NC)) * CAP + target % CAP
    head_normed, both, stream_parts, back = lax.optimization_barrier((head_normed, both, stream_parts, back))

    keep, give = project(pos, gather_line(head_normed, "x"), weights, tok_rows)
    own, *low = pair_sums(pos, keep, shift(give, "c", 1))
    parts = [shift(low[d - 1], "z", d) for d in range(1, NZ)]
    parts[0], stream_parts = lax.optimization_barrier((parts[0], stream_parts))
    stream_parts = stream_parts[:1] + [shift(stream_parts[d], "x", NX - d) for d in range(1, NX)]
    residual = quarter(pos, own, parts, stream_parts)
    quarters = gather_line(residual, "x")
    quarters[1], both = lax.optimization_barrier((quarters[1], both))
    targets = gather_line(both, "x")
    quarters[3], targets = lax.optimization_barrier((quarters[3], targets))
    normed, res = norm(pos, quarters, model_gain[None])
    message = place(pos, targets, normed, shift(normed, "c", 1))
    slot_rows = lax.all_to_all(
        message.reshape(NY * NZ, -1, D), ("y", "z"), split_axis=0, concat_axis=0, tiled=True
    ).reshape(slots, D)
    produced = run_expert(weight_scales, slot_rows, gate_weight[0], up_weight[0], down_weight[0])
    results = lax.all_to_all(
        produced.reshape(experts, CAP * BLOCKS, LANES), ("y", "z", "c", "x"), split_axis=0, concat_axis=0, tiled=True
    )
    return mix(back, expert_gates, results.reshape(slots, BLOCKS, LANES), res)


def solution(mesh):
    chips = jax.sharding.Mesh(mesh.devices.reshape(NX, NY, NZ, NC), AXES)
    seq, head = AXES[:2], AXES[2:]
    token = P(AXES, None)
    expert = P(AXES, None, None)
    return jax.shard_map(
        body,
        mesh=chips,
        in_specs=(
            P(seq, head),
            P(seq, head),
            P(seq, head),
            P(head),
            P(head, seq),
            token,
            P(),
            token,
            token,
            expert,
            expert,
            expert,
            token,
        ),
        out_specs=token,
        check_vma=False,
    )
```

```python
import jax
import jax.numpy as jnp
from jax import lax
from jax.experimental import pallas as pl
from jax.experimental.pallas import tpu as pltpu
from jax.sharding import PartitionSpec as P

D = 4096
HD = 128
TOPK = 8
CAP = 3
AXES = ("x", "y", "z", "c")
NX, NY, NZ, NC = 4, 4, 4, 2
LANES = 128
BLOCKS = D // LANES
DEEP = 512
OUT = 1024
BF = jnp.bfloat16
F32 = jnp.float32


SMEM = pl.BlockSpec(memory_space=pltpu.SMEM)
VMEM = pl.BlockSpec(memory_space=pltpu.VMEM)


def params(mib):
    return pltpu.CompilerParams(vmem_limit_bytes=mib << 20)


def cost(flops, size):
    return pl.CostEstimate(flops=flops, bytes_accessed=size, transcendentals=0)


def shift(a, axis, d):
    n = lax.axis_size(axis)
    return lax.ppermute(a, axis, [(i, (i + d) % n) for i in range(n)])


def gather_line(a, axis):
    n = lax.axis_size(axis)
    return [a] + [shift(a, axis, n - d) for d in range(1, n)]


def mixed_kernel(pos, query, before, one, two, three, local, gain, out):
    heads = before.shape[0]
    masks = [jnp.where(pos[0] >= d, 1.0, 0.0) for d in (1, 2, 3)]
    for h in range(heads):
        lanes = slice(h * HD, (h + 1) * HD)
        prior = before[h]
        for mask, got in zip(masks, (one, two, three)):
            prior += mask * got[h].astype(F32)
        mixed = local[:, lanes] + jnp.dot(query[:, lanes], prior.astype(BF), preferred_element_type=F32)
        mean_square = jnp.mean(mixed * mixed, axis=-1, keepdims=True)
        out[:, lanes] = (mixed * lax.rsqrt(mean_square + 1e-06) * gain[:, lanes]).astype(BF)


def mixed_heads(pos, query, before, totals, local, gain):
    return pl.pallas_call(
        mixed_kernel,
        out_shape=jax.ShapeDtypeStruct(query.shape, BF),
        in_specs=[SMEM] + [VMEM] * 7,
        out_specs=VMEM,
        compiler_params=params(16),
        cost_estimate=cost(1 << 25, 2 << 20),
    )(pos, query, before, *totals, local, gain)


def project_kernel(pos, *refs):
    tokens, weights, (keep, give, rows) = refs[:NX], refs[NX : NX + NY], refs[NX + NY :]
    tok, wide = keep.shape[1], weights[0].shape[1]
    mine = pl.multiple_of(pos[3] * tok, tok)
    other = pl.multiple_of(tok - pos[3] * tok, tok)
    for dx in range(NX):
        for dy in range(NY):
            rows[:, dy * wide : (dy + 1) * wide] = jnp.dot(
                tokens[dx][...], weights[dy][...], preferred_element_type=F32
            )
        for z in range(NZ):
            keep[dx * NZ + z] = rows[pl.ds(z * NC * tok + mine, tok), :]
            give[dx * NZ + z] = rows[pl.ds(z * NC * tok + other, tok), :].astype(BF)


def project(pos, tokens, weights, tok):
    wide = NY * weights[0].shape[1]
    shape = (NX * NZ, tok, wide)
    count, depth = tokens[0].shape
    return pl.pallas_call(
        project_kernel,
        out_shape=(jax.ShapeDtypeStruct(shape, F32), jax.ShapeDtypeStruct(shape, BF)),
        in_specs=[SMEM] + [VMEM] * (NX + NY),
        out_specs=(VMEM, VMEM),
        scratch_shapes=[pltpu.VMEM((count, wide), F32)],
        compiler_params=params(24),
        cost_estimate=cost(2 * NX * count * depth * wide, 5 << 20),
    )(pos, *tokens, *weights)


def pair_kernel(pos, keep, got, own, one, two, three):
    z = pos[2]
    for dx in range(NX):
        at = dx * NZ + z
        own[dx] = keep[at] + got[at].astype(F32)
        for d, out in ((1, one), (2, two), (3, three)):
            at = dx * NZ + lax.rem(z + d, NZ)
            out[dx] = (keep[at] + got[at].astype(F32)).astype(BF)


def pair_sums(pos, keep, got):
    shape = (NX, *keep.shape[1:])
    low = jax.ShapeDtypeStruct(shape, BF)
    return pl.pallas_call(
        pair_kernel,
        out_shape=(jax.ShapeDtypeStruct(shape, F32), low, low, low),
        in_specs=[SMEM, VMEM, VMEM],
        out_specs=(VMEM,) * 4,
        compiler_params=params(16),
        cost_estimate=cost(1 << 20, 5 << 20),
    )(pos, keep, got)


def quarter_kernel(pos, own, one, two, three, *refs):
    stream, out = refs[:NX], refs[NX]
    wide = 2 * LANES
    y = pos[1]
    for dx in range(NX):
        for dy in range(NY):
            lanes = slice(dy * wide, (dy + 1) * wide)
            at = pl.multiple_of(lax.rem(y + dy, NY) * wide, wide)
            total = (
                own[dx, :, lanes]
                + one[dx, :, lanes].astype(F32)
                + two[dx, :, lanes].astype(F32)
                + three[dx, :, lanes].astype(F32)
                + stream[dx][:, pl.ds(at, wide)].astype(F32)
            )
            out[dx, :, pl.ds(at, wide)] = total.astype(BF)


def quarter(pos, own, parts, stream):
    return pl.pallas_call(
        quarter_kernel,
        out_shape=jax.ShapeDtypeStruct(own.shape, BF),
        in_specs=[SMEM] + [VMEM] * (NZ + NX),
        out_specs=VMEM,
        compiler_params=params(16),
        cost_estimate=cost(1 << 20, 3 << 20),
    )(pos, own, *parts, *stream)


def norm_kernel(pos, *refs):
    quarters, gain, normed, res = refs[:NX], refs[NX], refs[NX + 1], refs[NX + 2]
    tok, wide = quarters[0].shape[1:]
    x = pos[0]
    at = [pl.multiple_of(lax.rem(x + d, NX) * wide, wide) for d in range(NX)]
    for b in range(NX):
        values = [quarters[d][(b - d) % NX].astype(F32) for d in range(NX)]
        squares = values[0] * values[0]
        for value in values[1:]:
            squares += value * value
        factor = lax.rsqrt(jnp.sum(squares, axis=1, keepdims=True) * (1.0 / D) + 1e-06)
        for d in range(NX):
            lanes = pl.ds(at[d], wide)
            normed[b * tok : (b + 1) * tok, lanes] = (values[d] * factor * gain[:, lanes]).astype(BF)
            if b == 0:
                res[:, lanes] = values[d].astype(BF)


def norm(pos, quarters, gain):
    tok = quarters[0].shape[1]
    return pl.pallas_call(
        norm_kernel,
        out_shape=(jax.ShapeDtypeStruct((NX * tok, D), BF), jax.ShapeDtypeStruct((tok, D), BF)),
        in_specs=[SMEM] + [VMEM] * (NX + 1),
        out_specs=(VMEM, VMEM),
        compiler_params=params(16),
        cost_estimate=cost(1 << 21, 3 << 20),
    )(pos, *quarters, gain)


def places_kernel(pos, *refs):
    parts, where = refs[:NX], refs[NX]
    x, c = pos[0], pos[3]
    slots, tok = where.shape[0], parts[0].shape[0]
    row = lax.broadcasted_iota(jnp.int32, (slots, tok), 0)
    block = row // CAP % (NC * NX)
    wanted = ((x * NY * NZ + row // (NC * NX * CAP)) * NC + c) * CAP + row % CAP
    wanted = wanted.astype(F32)
    for d in range(NX):
        choice = parts[d][:, D // NX :].astype(F32).T
        for core in range(NC):
            at = 2 * core * TOPK
            target = choice[at : at + TOPK] * CAP + choice[at + TOPK : at + 2 * TOPK]
            mine = block == lax.rem(c + core, NC) * NX + lax.rem(x + d, NX)
            found = jnp.zeros((slots, tok), jnp.bool_)
            for k in range(TOPK):
                found |= target[k : k + 1] == wanted
            piece = core * NX + d
            where[:, piece * tok : (piece + 1) * tok] = jnp.where(mine & found, 1.0, 0.0).astype(BF)


def find_places(pos, parts):
    slots, tokens = NX * NY * NZ * NC * CAP, NC * NX * parts[0].shape[0]
    return pl.pallas_call(
        places_kernel,
        out_shape=jax.ShapeDtypeStruct((slots, tokens), BF),
        in_specs=[SMEM] + [VMEM] * NX,
        out_specs=VMEM,
        compiler_params=params(8),
        cost_estimate=cost(1 << 21, 1 << 18),
    )(pos, *parts)


def place_kernel(where, own, other, message):
    tokens = own.shape[0]
    for j in range(0, D, OUT):
        lanes = slice(j, j + OUT)
        total = jnp.dot(where[:, :tokens], own[:, lanes], preferred_element_type=F32)
        total += jnp.dot(where[:, tokens:], other[:, lanes], preferred_element_type=F32)
        message[:, lanes] = total.astype(BF)


def place(where, own, other):
    return pl.pallas_call(
        place_kernel,
        out_shape=jax.ShapeDtypeStruct((where.shape[0], D), BF),
        in_specs=[VMEM] * 3,
        out_specs=VMEM,
        compiler_params=params(16),
        cost_estimate=cost(2 * where.shape[0] * where.shape[1] * D, 5 << 20),
    )(where, own, other)


def expert_kernel(scale, rows, gate, up, down, out, x, wg, wu, wd, gates, ups, act, part, done, in_sem, down_sem, out_sem):
    depth, hidden = wg.shape
    groups = OUT // LANES
    loads, downs, stores = [], [], []
    for i, j in enumerate(range(0, depth, DEEP)):
        at = pl.ds(j, DEEP)
        for k, (source, into) in enumerate(((rows, x), (gate, wg), (up, wu))):
            view = (source.at[:, at], into.at[:, at]) if k == 0 else (source.at[at], into.at[at])
            loads.append(pltpu.make_async_copy(*view, in_sem.at[3 * i + k]))
            loads[-1].start()
    for i, j in enumerate(range(0, depth, OUT)):
        at = pl.ds(j, OUT)
        downs.append(pltpu.make_async_copy(down.at[:, at], wd.at[:, at], down_sem.at[i]))
        downs[-1].start()
    for i, j in enumerate(range(0, depth, DEEP)):
        for load in loads[3 * i : 3 * i + 3]:
            load.wait()
        cut = x[:, j : j + DEEP]
        gate_part = jnp.dot(cut, wg[j : j + DEEP], preferred_element_type=F32)
        up_part = jnp.dot(cut, wu[j : j + DEEP], preferred_element_type=F32)
        if i == 0:
            gates[...] = gate_part
            ups[...] = up_part
        else:
            gates[...] += gate_part
            ups[...] += up_part
    gate_part = gates[...] * scale[0, 0]
    act[...] = (gate_part / (1.0 + jnp.exp(-gate_part)) * (ups[...] * scale[0, 1])).astype(BF)
    for load in downs:
        load.wait()
    for i, j in enumerate(range(0, depth, OUT)):
        total = jnp.dot(act[...], wd[:, j : j + OUT], preferred_element_type=F32) * scale[0, 2]
        two, first = i // 2, i % 2 * groups
        for g in range(groups):
            part[two % 2, :, first + g, :] = total[:, g * LANES : (g + 1) * LANES]
        if first:
            at = pl.ds(two * 2 * groups, 2 * groups)
            done[:, at, :] = part[two % 2].astype(BF)
            stores.append(pltpu.make_async_copy(done.at[:, at, :], out.at[:, at, :], out_sem.at[two]))
            stores[-1].start()
    for store in stores:
        store.wait()


def run_expert(scale, rows, gate, up, down):
    count, depth = rows.shape
    hidden = gate.shape[1]
    anywhere = pl.BlockSpec(memory_space=pl.ANY)
    return pl.pallas_call(
        expert_kernel,
        out_shape=jax.ShapeDtypeStruct((count, BLOCKS, LANES), BF),
        in_specs=[SMEM] + [anywhere] * 4,
        out_specs=anywhere,
        scratch_shapes=[
            pltpu.VMEM((count, depth), BF),
            pltpu.VMEM((depth, hidden), BF),
            pltpu.VMEM((depth, hidden), BF),
            pltpu.VMEM((hidden, depth), BF),
            pltpu.VMEM((count, hidden), F32),
            pltpu.VMEM((count, hidden), F32),
            pltpu.VMEM((count, hidden), BF),
            pltpu.VMEM((2, count, 2 * OUT // LANES, LANES), F32),
            pltpu.VMEM((count, BLOCKS, LANES), BF),
            pltpu.SemaphoreType.DMA((3 * depth // DEEP,)),
            pltpu.SemaphoreType.DMA((depth // OUT,)),
            pltpu.SemaphoreType.DMA((depth // (2 * OUT),)),
        ],
        compiler_params=params(58),
        cost_estimate=cost(6 * count * depth * hidden, 6 * depth * hidden),
    )(scale, rows, gate, up, down)


def mix_kernel(target, gates, results, res, out, mixed):
    tok = res.shape[0]

    def one_token(t, carry):
        add = gates[t, 0] * results[target[t, 0]].astype(F32)
        for k in range(1, TOPK):
            add += gates[t, k] * results[target[t, k]].astype(F32)
        mixed[t] = add
        return carry

    lax.fori_loop(0, tok, one_token, 0)
    for block in range(BLOCKS):
        lanes = slice(block * LANES, (block + 1) * LANES)
        out[:, lanes] = (res[:, lanes].astype(F32) + mixed[:, block, :]).astype(BF)


def mix(target, gates, results, res):
    tok = res.shape[0]
    return pl.pallas_call(
        mix_kernel,
        out_shape=jax.ShapeDtypeStruct((tok, D), BF),
        in_specs=[SMEM, SMEM, VMEM, VMEM],
        out_specs=VMEM,
        scratch_shapes=[pltpu.VMEM((tok, BLOCKS, LANES), F32)],
        compiler_params=params(16),
        cost_estimate=cost(1 << 20, 4 << 20),
    )(target, gates, results, res)


def body(
    query,
    key,
    value,
    head_gain,
    out_weight,
    stream,
    model_gain,
    expert_ids,
    expert_gates,
    gate_weight,
    up_weight,
    down_weight,
    weight_scales,
):
    x, y, z, c = [lax.axis_index(axis) for axis in AXES]
    pos = jnp.stack([x, y, z, c]).astype(jnp.int32)
    seq_rows = query.shape[0]
    tok_rows = stream.shape[0]
    heads_local = head_gain.shape[0] // HD
    experts = NX * NY * NZ * NC
    slots = experts * CAP

    query_rows = query.reshape(seq_rows, heads_local, HD)
    key_rows = key.reshape(seq_rows, heads_local, HD)
    value_rows = value.reshape(seq_rows, heads_local, HD)
    block_state = jnp.einsum("shd,she->hde", key_rows, value_rows, preferred_element_type=F32)
    low = block_state.astype(BF)
    line, before = block_state, jnp.zeros_like(block_state)
    for d in range(1, NY):
        got = shift(low, "y", d).astype(F32)
        line = line + got
        before = before + jnp.where(y >= d, got, 0.0)
    low = line.astype(BF)
    totals = [shift(low, "x", d) for d in range(1, NX)]
    weights = gather_line(out_weight, "y")

    scores = jnp.einsum("thd,shd->hts", query_rows, key_rows, preferred_element_type=F32)
    causal = jnp.tril(jnp.ones((seq_rows, seq_rows), dtype=bool))
    scores = jnp.where(causal[None, :, :], scores, 0.0).astype(BF)
    local_part = jnp.einsum("hts,shd->thd", scores, value_rows, preferred_element_type=F32)
    local_part = local_part.reshape(seq_rows, heads_local * HD)
    head_normed = mixed_heads(pos, query, before, totals, local_part, head_gain[None])

    flat_ids = expert_ids.reshape(-1)
    at = jnp.arange(flat_ids.shape[0], dtype=jnp.int32)
    same = (flat_ids[:, None] == flat_ids[None, :]) & (at[None, :] < at[:, None])
    slot_index = jnp.sum(same.astype(jnp.int32), axis=1)
    target = (flat_ids * CAP + slot_index).reshape(tok_rows, TOPK)

    own_choice = jnp.concatenate([expert_ids, slot_index.reshape(tok_rows, TOPK)], axis=1).astype(BF)
    choice = jnp.concatenate([own_choice, shift(own_choice, "c", 1)], axis=1)
    choice = jnp.pad(choice, ((0, 0), (0, LANES - choice.shape[1])))
    wide = D // NX
    stream_parts = [
        jnp.concatenate(
            [lax.dynamic_slice_in_dim(stream, (x + NX - d) % NX * wide, wide, axis=1), choice], axis=1
        )
        for d in range(NX)
    ]
    back = target // CAP
    back = (back % (NY * NZ * NC) * NX + back // (NY * NZ * NC)) * CAP + target % CAP
    head_normed, stream_parts, back = lax.optimization_barrier((head_normed, stream_parts, back))

    keep, give = project(pos, gather_line(head_normed, "x"), weights, tok_rows)
    own, *low = pair_sums(pos, keep, shift(give, "c", 1))
    parts = [shift(low[d - 1], "z", d) for d in range(1, NZ)]
    parts[0], stream_parts = lax.optimization_barrier((parts[0], stream_parts))
    stream_parts = stream_parts[:1] + [shift(stream_parts[d], "x", NX - d) for d in range(1, NX)]
    residual = quarter(pos, own, parts, stream_parts)
    quarters = gather_line(residual, "x")
    where = find_places(pos, stream_parts)
    quarters[3], where = lax.optimization_barrier((quarters[3], where))
    normed, res = norm(pos, quarters, model_gain[None])
    message = place(where, normed, shift(normed, "c", 1))
    slot_rows = lax.all_to_all(
        message.reshape(NY * NZ, -1, D), ("y", "z"), split_axis=0, concat_axis=0, tiled=True
    ).reshape(slots, D)
    produced = run_expert(weight_scales, slot_rows, gate_weight[0], up_weight[0], down_weight[0])
    results = lax.all_to_all(
        produced.reshape(experts, CAP * BLOCKS, LANES), ("y", "z", "c", "x"), split_axis=0, concat_axis=0, tiled=True
    )
    return mix(back, expert_gates, results.reshape(slots, BLOCKS, LANES), res)


def solution(mesh):
    chips = jax.sharding.Mesh(mesh.devices.reshape(NX, NY, NZ, NC), AXES)
    seq, head = AXES[:2], AXES[2:]
    token = P(AXES, None)
    expert = P(AXES, None, None)
    return jax.shard_map(
        body,
        mesh=chips,
        in_specs=(
            P(seq, head),
            P(seq, head),
            P(seq, head),
            P(head),
            P(head, seq),
            token,
            P(),
            token,
            token,
            expert,
            expert,
            expert,
            token,
        ),
        out_specs=token,
        check_vma=False,
    )
```

```python
import jax
import jax.numpy as jnp
from jax import lax
from jax.experimental import pallas as pl
from jax.experimental.pallas import tpu as pltpu
from jax.sharding import PartitionSpec as P

D = 4096
HD = 128
TOPK = 8
CAP = 3
NX, NY, NZ, NC = 4, 4, 4, 2
LANES = 128
BLOCKS = D // LANES
DEEP = 512
OUT = 1024
BF = jnp.bfloat16
F32 = jnp.float32


SMEM = pl.BlockSpec(memory_space=pltpu.SMEM)
VMEM = pl.BlockSpec(memory_space=pltpu.VMEM)


def params(mib):
    return pltpu.CompilerParams(vmem_limit_bytes=mib << 20)


def cost(flops, size):
    return pl.CostEstimate(flops=flops, bytes_accessed=size, transcendentals=0)


def to_x(a, d):
    pairs = [(x * NY + y, (x + d) % NX * NY + y) for x in range(NX) for y in range(NY)]
    return lax.ppermute(a, "seq", pairs)


def to_y(a, d):
    pairs = [(x * NY + y, x * NY + (y + d) % NY) for x in range(NX) for y in range(NY)]
    return lax.ppermute(a, "seq", pairs)


def to_z(a, d):
    pairs = [(z * NC + c, (z + d) % NZ * NC + c) for z in range(NZ) for c in range(NC)]
    return lax.ppermute(a, "head", pairs)


def swap_core(a):
    pairs = [(z * NC + c, z * NC + 1 - c) for z in range(NZ) for c in range(NC)]
    return lax.ppermute(a, "head", pairs)


def mixed_kernel(pos, query, before, one, two, three, local, gain, out):
    heads = before.shape[0]
    masks = [jnp.where(pos[0] >= d, 1.0, 0.0) for d in (1, 2, 3)]
    for h in range(heads):
        lanes = slice(h * HD, (h + 1) * HD)
        prior = before[h]
        for mask, got in zip(masks, (one, two, three)):
            prior += mask * got[h].astype(F32)
        mixed = local[:, lanes] + jnp.dot(query[:, lanes], prior.astype(BF), preferred_element_type=F32)
        mean_square = jnp.mean(mixed * mixed, axis=-1, keepdims=True)
        out[:, lanes] = (mixed * lax.rsqrt(mean_square + 1e-06) * gain[:, lanes]).astype(BF)


def mixed_heads(pos, query, before, totals, local, gain):
    return pl.pallas_call(
        mixed_kernel,
        out_shape=jax.ShapeDtypeStruct(query.shape, BF),
        in_specs=[SMEM] + [VMEM] * 7,
        out_specs=VMEM,
        compiler_params=params(16),
        cost_estimate=cost(1 << 25, 2 << 20),
    )(pos, query, before, *totals, local, gain)


def project_kernel(pos, *refs):
    tokens, weights, (keep, give, rows) = refs[:NX], refs[NX : NX + NY], refs[NX + NY :]
    tok, wide = keep.shape[1], weights[0].shape[1]
    mine = pl.multiple_of(pos[3] * tok, tok)
    other = pl.multiple_of(tok - pos[3] * tok, tok)
    for dx in range(NX):
        for dy in range(NY):
            rows[:, dy * wide : (dy + 1) * wide] = jnp.dot(
                tokens[dx][...], weights[dy][...], preferred_element_type=F32
            )
        for z in range(NZ):
            keep[dx * NZ + z] = rows[pl.ds(z * NC * tok + mine, tok), :]
            give[dx * NZ + z] = rows[pl.ds(z * NC * tok + other, tok), :].astype(BF)


def project(pos, tokens, weights, tok):
    wide = NY * weights[0].shape[1]
    shape = (NX * NZ, tok, wide)
    count, depth = tokens[0].shape
    return pl.pallas_call(
        project_kernel,
        out_shape=(jax.ShapeDtypeStruct(shape, F32), jax.ShapeDtypeStruct(shape, BF)),
        in_specs=[SMEM] + [VMEM] * (NX + NY),
        out_specs=(VMEM, VMEM),
        scratch_shapes=[pltpu.VMEM((count, wide), F32)],
        compiler_params=params(24),
        cost_estimate=cost(2 * NX * count * depth * wide, 5 << 20),
    )(pos, *tokens, *weights)


def pair_kernel(pos, keep, got, own, one, two, three):
    z = pos[2]
    for dx in range(NX):
        at = dx * NZ + z
        own[dx] = keep[at] + got[at].astype(F32)
        for d, out in ((1, one), (2, two), (3, three)):
            at = dx * NZ + lax.rem(z + d, NZ)
            out[dx] = (keep[at] + got[at].astype(F32)).astype(BF)


def pair_sums(pos, keep, got):
    shape = (NX, *keep.shape[1:])
    low = jax.ShapeDtypeStruct(shape, BF)
    return pl.pallas_call(
        pair_kernel,
        out_shape=(jax.ShapeDtypeStruct(shape, F32), low, low, low),
        in_specs=[SMEM, VMEM, VMEM],
        out_specs=(VMEM,) * 4,
        compiler_params=params(16),
        cost_estimate=cost(1 << 20, 5 << 20),
    )(pos, keep, got)


def sum_kernel(own, one, two, three, *outs):
    for dx, out in enumerate(outs):
        total = own[dx] + one[dx].astype(F32) + two[dx].astype(F32) + three[dx].astype(F32)
        out[...] = total.astype(out.dtype)


def sum_z(own, parts):
    shape = own.shape[1:]
    low = jax.ShapeDtypeStruct(shape, BF)
    return pl.pallas_call(
        sum_kernel,
        out_shape=(jax.ShapeDtypeStruct(shape, F32), low, low, low),
        in_specs=[VMEM] * NZ,
        out_specs=(VMEM,) * NX,
        compiler_params=params(16),
        cost_estimate=cost(1 << 20, 2 << 20),
    )(own, *parts)


def place_kernel(pos, target, own, one, two, three, stream, gain, res, message, total, scaled):
    tok = own.shape[0]
    wide = 2 * LANES
    x, y = pos[0], pos[1]
    squares = jnp.zeros((tok, LANES), F32)
    places = []
    for dx, part in enumerate((own, one, two, three)):
        for dy in range(NY):
            seq = lax.rem(x + NX - dx, NX) * NY + lax.rem(y + dy, NY)
            at = pl.multiple_of(seq * wide, wide)
            value = part[:, dy * wide : (dy + 1) * wide].astype(F32) + stream[:, pl.ds(at, wide)].astype(F32)
            value = value.astype(BF).astype(F32)
            j = dx * NY + dy
            total[:, j * wide : (j + 1) * wide] = value
            for half in range(2):
                cut = value[:, half * LANES : (half + 1) * LANES]
                squares += cut * cut
                res[:, pl.ds(seq * 2 + half, 1), :] = cut[:, None, :]
            places.append((j, seq, at))
    factor = lax.rsqrt(jnp.sum(squares, axis=1, keepdims=True) * (1.0 / D) + 1e-06)
    for j, seq, at in places:
        value = total[:, j * wide : (j + 1) * wide] * factor * gain[:, pl.ds(at, wide)]
        for half in range(2):
            scaled[:, pl.ds(seq * 2 + half, 1), :] = value[:, half * LANES : (half + 1) * LANES][:, None, :]
    message[...] = jnp.zeros_like(message)

    def one_token(t, carry):
        row = scaled[t].astype(BF)
        for k in range(TOPK):
            message[target[t, k]] = row
        return carry

    lax.fori_loop(0, tok, one_token, 0)


def place(pos, target, parts, stream, gain, slots):
    tok = stream.shape[0]
    return pl.pallas_call(
        place_kernel,
        out_shape=(
            jax.ShapeDtypeStruct((tok, BLOCKS, LANES), F32),
            jax.ShapeDtypeStruct((slots, BLOCKS, LANES), BF),
        ),
        in_specs=[SMEM, SMEM] + [VMEM] * 6,
        out_specs=(VMEM, VMEM),
        scratch_shapes=[pltpu.VMEM((tok, D), F32), pltpu.VMEM((tok, BLOCKS, LANES), F32)],
        compiler_params=params(24),
        cost_estimate=cost(1 << 20, 5 << 20),
    )(pos, target, *parts, stream, gain)


def expert_kernel(scale, rows, gate, up, down, out, x, wg, wu, wd, gates, ups, act, part, done, in_sem, down_sem, out_sem):
    depth, hidden = wg.shape
    groups = OUT // LANES
    loads, downs, stores = [], [], []
    for i, j in enumerate(range(0, depth, DEEP)):
        at = pl.ds(j, DEEP)
        for k, (source, into) in enumerate(((rows, x), (gate, wg), (up, wu))):
            view = (source.at[:, at], into.at[:, at]) if k == 0 else (source.at[at], into.at[at])
            loads.append(pltpu.make_async_copy(*view, in_sem.at[3 * i + k]))
            loads[-1].start()
    for i, j in enumerate(range(0, depth, OUT)):
        at = pl.ds(j, OUT)
        downs.append(pltpu.make_async_copy(down.at[:, at], wd.at[:, at], down_sem.at[i]))
        downs[-1].start()
    for i, j in enumerate(range(0, depth, DEEP)):
        for load in loads[3 * i : 3 * i + 3]:
            load.wait()
        cut = x[:, j : j + DEEP]
        gate_part = jnp.dot(cut, wg[j : j + DEEP], preferred_element_type=F32)
        up_part = jnp.dot(cut, wu[j : j + DEEP], preferred_element_type=F32)
        if i == 0:
            gates[...] = gate_part
            ups[...] = up_part
        else:
            gates[...] += gate_part
            ups[...] += up_part
    gate_part = gates[...] * scale[0, 0]
    act[...] = (gate_part / (1.0 + jnp.exp(-gate_part)) * (ups[...] * scale[0, 1])).astype(BF)
    for load in downs:
        load.wait()
    for i, j in enumerate(range(0, depth, OUT)):
        total = jnp.dot(act[...], wd[:, j : j + OUT], preferred_element_type=F32) * scale[0, 2]
        two, first = i // 2, i % 2 * groups
        for g in range(groups):
            part[two % 2, :, first + g, :] = total[:, g * LANES : (g + 1) * LANES]
        if first:
            at = pl.ds(two * 2 * groups, 2 * groups)
            done[:, at, :] = part[two % 2].astype(BF)
            stores.append(pltpu.make_async_copy(done.at[:, at, :], out.at[:, at, :], out_sem.at[two]))
            stores[-1].start()
    for store in stores:
        store.wait()


def run_expert(scale, rows, gate, up, down):
    count, depth = rows.shape
    hidden = gate.shape[1]
    anywhere = pl.BlockSpec(memory_space=pl.ANY)
    return pl.pallas_call(
        expert_kernel,
        out_shape=jax.ShapeDtypeStruct((count, BLOCKS, LANES), BF),
        in_specs=[SMEM] + [anywhere] * 4,
        out_specs=anywhere,
        scratch_shapes=[
            pltpu.VMEM((count, depth), BF),
            pltpu.VMEM((depth, hidden), BF),
            pltpu.VMEM((depth, hidden), BF),
            pltpu.VMEM((hidden, depth), BF),
            pltpu.VMEM((count, hidden), F32),
            pltpu.VMEM((count, hidden), F32),
            pltpu.VMEM((count, hidden), BF),
            pltpu.VMEM((2, count, 2 * OUT // LANES, LANES), F32),
            pltpu.VMEM((count, BLOCKS, LANES), BF),
            pltpu.SemaphoreType.DMA((3 * depth // DEEP,)),
            pltpu.SemaphoreType.DMA((depth // OUT,)),
            pltpu.SemaphoreType.DMA((depth // (2 * OUT),)),
        ],
        compiler_params=params(58),
        cost_estimate=cost(6 * count * depth * hidden, 6 * depth * hidden),
    )(scale, rows, gate, up, down)


def mix_kernel(target, gates, results, res, out, mixed):
    tok = res.shape[0]

    def one_token(t, carry):
        add = gates[t, 0] * results[target[t, 0]].astype(F32)
        for k in range(1, TOPK):
            add += gates[t, k] * results[target[t, k]].astype(F32)
        mixed[t] = res[t] + add
        return carry

    lax.fori_loop(0, tok, one_token, 0)
    for block in range(BLOCKS):
        out[:, block * LANES : (block + 1) * LANES] = mixed[:, block, :].astype(BF)


def mix(target, gates, results, res):
    tok = res.shape[0]
    return pl.pallas_call(
        mix_kernel,
        out_shape=jax.ShapeDtypeStruct((tok, D), BF),
        in_specs=[SMEM, SMEM, VMEM, VMEM],
        out_specs=VMEM,
        scratch_shapes=[pltpu.VMEM(res.shape, F32)],
        compiler_params=params(16),
        cost_estimate=cost(1 << 20, 4 << 20),
    )(target, gates, results, res)


def body(
    query,
    key,
    value,
    head_gain,
    out_weight,
    stream,
    model_gain,
    expert_ids,
    expert_gates,
    gate_weight,
    up_weight,
    down_weight,
    weight_scales,
):
    seq = lax.axis_index("seq")
    head = lax.axis_index("head")
    x, y, z, c = seq // NY, seq % NY, head // NC, head % NC
    pos = jnp.stack([x, y, z, c]).astype(jnp.int32)
    seq_rows = query.shape[0]
    tok_rows = stream.shape[0]
    heads_local = head_gain.shape[0] // HD
    experts = lax.axis_size("seq") * lax.axis_size("head")
    slots = experts * CAP

    query_rows = query.reshape(seq_rows, heads_local, HD)
    key_rows = key.reshape(seq_rows, heads_local, HD)
    value_rows = value.reshape(seq_rows, heads_local, HD)
    block_state = jnp.einsum("shd,she->hde", key_rows, value_rows, preferred_element_type=F32)
    low = block_state.astype(BF)
    line, before = block_state, jnp.zeros_like(block_state)
    for d in range(1, NY):
        got = to_y(low, d).astype(F32)
        line = line + got
        before = before + jnp.where(y >= d, got, 0.0)
    low = line.astype(BF)
    totals = [to_x(low, d) for d in range(1, NX)]
    weights = [out_weight] + [to_y(out_weight, NY - d) for d in range(1, NY)]

    scores = jnp.einsum("thd,shd->hts", query_rows, key_rows, preferred_element_type=F32)
    causal = jnp.tril(jnp.ones((seq_rows, seq_rows), dtype=bool))
    scores = jnp.where(causal[None, :, :], scores, 0.0).astype(BF)
    local_part = jnp.einsum("hts,shd->thd", scores, value_rows, preferred_element_type=F32)
    local_part = local_part.reshape(seq_rows, heads_local * HD)
    head_normed = mixed_heads(pos, query, before, totals, local_part, head_gain[None])

    flat_ids = expert_ids.reshape(-1)
    at = jnp.arange(flat_ids.shape[0], dtype=jnp.int32)
    same = (flat_ids[:, None] == flat_ids[None, :]) & (at[None, :] < at[:, None])
    slot_index = jnp.sum(same.astype(jnp.int32), axis=1)
    target = (flat_ids * CAP + slot_index).reshape(tok_rows, TOPK)

    def exchange(rows):
        message = rows.reshape(experts, CAP * BLOCKS, LANES)
        got = lax.all_to_all(message, ("seq", "head"), split_axis=0, concat_axis=0, tiled=True)
        return got.reshape(slots, BLOCKS, LANES)

    tokens = [head_normed] + [to_x(head_normed, NX - d) for d in range(1, NX)]
    keep, give = project(pos, tokens, weights, tok_rows)
    own, *low = pair_sums(pos, keep, swap_core(give))
    sums = sum_z(own, [to_z(low[d - 1], d) for d in range(1, NZ)])
    parts = [sums[0]] + [to_x(sums[d], d) for d in range(1, NX)]
    res, message = place(pos, target, parts, stream, model_gain[None], slots)
    slot_rows = exchange(message).reshape(slots, D)
    produced = run_expert(weight_scales, slot_rows, gate_weight[0], up_weight[0], down_weight[0])
    results = exchange(produced)
    return mix(target, expert_gates, results, res)


def solution(mesh):
    token = P(("seq", "head"), None)
    expert = P(("seq", "head"), None, None)
    return jax.shard_map(
        body,
        mesh=mesh,
        in_specs=(
            P("seq", "head"),
            P("seq", "head"),
            P("seq", "head"),
            P("head"),
            P("head", "seq"),
            token,
            P(),
            token,
            token,
            expert,
            expert,
            expert,
            token,
        ),
        out_specs=token,
        check_vma=False,
    )
```

```python
import jax
import jax.numpy as jnp
from jax import lax
from jax.experimental import pallas as pl
from jax.experimental.pallas import tpu as pltpu
from jax.sharding import PartitionSpec as P

D = 4096
HD = 128
TOPK = 8
CAP = 3
NX, NY, NZ, NC = 4, 4, 4, 2
LANES = 128
BLOCKS = D // LANES
DEEP = 512
OUT = 1024
BF = jnp.bfloat16
F32 = jnp.float32


SMEM = pl.BlockSpec(memory_space=pltpu.SMEM)
VMEM = pl.BlockSpec(memory_space=pltpu.VMEM)


def params(mib):
    return pltpu.CompilerParams(vmem_limit_bytes=mib << 20)


def cost(flops, size):
    return pl.CostEstimate(flops=flops, bytes_accessed=size, transcendentals=0)


def to_x(a, d):
    pairs = [(x * NY + y, (x + d) % NX * NY + y) for x in range(NX) for y in range(NY)]
    return lax.ppermute(a, "seq", pairs)


def to_y(a, d):
    pairs = [(x * NY + y, x * NY + (y + d) % NY) for x in range(NX) for y in range(NY)]
    return lax.ppermute(a, "seq", pairs)


def to_z(a, d):
    pairs = [(z * NC + c, (z + d) % NZ * NC + c) for z in range(NZ) for c in range(NC)]
    return lax.ppermute(a, "head", pairs)


def swap_core(a):
    pairs = [(z * NC + c, z * NC + 1 - c) for z in range(NZ) for c in range(NC)]
    return lax.ppermute(a, "head", pairs)


def mixed_kernel(pos, query, before, one, two, three, local, gain, out):
    heads = before.shape[0]
    masks = [jnp.where(pos[0] >= d, 1.0, 0.0) for d in (1, 2, 3)]
    for h in range(heads):
        lanes = slice(h * HD, (h + 1) * HD)
        prior = before[h]
        for mask, got in zip(masks, (one, two, three)):
            prior += mask * got[h].astype(F32)
        mixed = local[:, lanes] + jnp.dot(query[:, lanes], prior.astype(BF), preferred_element_type=F32)
        mean_square = jnp.mean(mixed * mixed, axis=-1, keepdims=True)
        out[:, lanes] = (mixed * lax.rsqrt(mean_square + 1e-06) * gain[:, lanes]).astype(BF)


def mixed_heads(pos, query, before, totals, local, gain):
    return pl.pallas_call(
        mixed_kernel,
        out_shape=jax.ShapeDtypeStruct(query.shape, BF),
        in_specs=[SMEM] + [VMEM] * 7,
        out_specs=VMEM,
        compiler_params=params(16),
        cost_estimate=cost(1 << 25, 2 << 20),
    )(pos, query, before, *totals, local, gain)


def project_kernel(pos, *refs):
    tokens, weights, (keep, give, rows) = refs[:NX], refs[NX : NX + NY], refs[NX + NY :]
    tok, wide = keep.shape[1], weights[0].shape[1]
    mine = pl.multiple_of(pos[3] * tok, tok)
    other = pl.multiple_of(tok - pos[3] * tok, tok)
    for dx in range(NX):
        for dy in range(NY):
            rows[:, dy * wide : (dy + 1) * wide] = jnp.dot(
                tokens[dx][...], weights[dy][...], preferred_element_type=F32
            )
        for z in range(NZ):
            keep[dx * NZ + z] = rows[pl.ds(z * NC * tok + mine, tok), :]
            give[dx * NZ + z] = rows[pl.ds(z * NC * tok + other, tok), :].astype(BF)


def project(pos, tokens, weights, tok):
    wide = NY * weights[0].shape[1]
    shape = (NX * NZ, tok, wide)
    count, depth = tokens[0].shape
    return pl.pallas_call(
        project_kernel,
        out_shape=(jax.ShapeDtypeStruct(shape, F32), jax.ShapeDtypeStruct(shape, BF)),
        in_specs=[SMEM] + [VMEM] * (NX + NY),
        out_specs=(VMEM, VMEM),
        scratch_shapes=[pltpu.VMEM((count, wide), F32)],
        compiler_params=params(24),
        cost_estimate=cost(2 * NX * count * depth * wide, 5 << 20),
    )(pos, *tokens, *weights)


def pair_kernel(pos, keep, got, own, one, two, three):
    z = pos[2]
    for dx in range(NX):
        at = dx * NZ + z
        own[dx] = keep[at] + got[at].astype(F32)
        for d, out in ((1, one), (2, two), (3, three)):
            at = dx * NZ + lax.rem(z + d, NZ)
            out[dx] = (keep[at] + got[at].astype(F32)).astype(BF)


def pair_sums(pos, keep, got):
    shape = (NX, *keep.shape[1:])
    low = jax.ShapeDtypeStruct(shape, BF)
    return pl.pallas_call(
        pair_kernel,
        out_shape=(jax.ShapeDtypeStruct(shape, F32), low, low, low),
        in_specs=[SMEM, VMEM, VMEM],
        out_specs=(VMEM,) * 4,
        compiler_params=params(16),
        cost_estimate=cost(1 << 20, 5 << 20),
    )(pos, keep, got)


def sum_kernel(own, one, two, three, *outs):
    for dx, out in enumerate(outs):
        total = own[dx] + one[dx].astype(F32) + two[dx].astype(F32) + three[dx].astype(F32)
        out[...] = total.astype(out.dtype)


def sum_z(own, parts):
    shape = own.shape[1:]
    low = jax.ShapeDtypeStruct(shape, BF)
    return pl.pallas_call(
        sum_kernel,
        out_shape=(jax.ShapeDtypeStruct(shape, F32), low, low, low),
        in_specs=[VMEM] * NZ,
        out_specs=(VMEM,) * NX,
        compiler_params=params(16),
        cost_estimate=cost(1 << 20, 2 << 20),
    )(own, *parts)


def place_kernel(pos, target, own, one, two, three, stream, gain, res, message, total, scaled):
    tok = own.shape[0]
    wide = 2 * LANES
    x, y = pos[0], pos[1]
    squares = jnp.zeros((tok, LANES), F32)
    places = []
    for dx, part in enumerate((own, one, two, three)):
        for dy in range(NY):
            seq = lax.rem(x + NX - dx, NX) * NY + lax.rem(y + dy, NY)
            at = pl.multiple_of(seq * wide, wide)
            value = part[:, dy * wide : (dy + 1) * wide].astype(F32) + stream[:, pl.ds(at, wide)].astype(F32)
            value = value.astype(BF).astype(F32)
            j = dx * NY + dy
            total[:, j * wide : (j + 1) * wide] = value
            res[:, pl.ds(at, wide)] = value.astype(BF)
            for half in range(2):
                cut = value[:, half * LANES : (half + 1) * LANES]
                squares += cut * cut
            places.append((j, seq, at))
    factor = lax.rsqrt(jnp.sum(squares, axis=1, keepdims=True) * (1.0 / D) + 1e-06)
    for j, seq, at in places:
        value = total[:, j * wide : (j + 1) * wide] * factor * gain[:, pl.ds(at, wide)]
        for half in range(2):
            scaled[:, pl.ds(seq * 2 + half, 1), :] = value[:, half * LANES : (half + 1) * LANES][:, None, :]
    message[...] = jnp.zeros_like(message)

    def one_token(t, carry):
        row = scaled[t].astype(BF)
        for k in range(TOPK):
            message[target[t, k]] = row
        return carry

    lax.fori_loop(0, tok, one_token, 0)


def place(pos, target, parts, stream, gain, slots):
    tok = stream.shape[0]
    return pl.pallas_call(
        place_kernel,
        out_shape=(
            jax.ShapeDtypeStruct((tok, D), BF),
            jax.ShapeDtypeStruct((slots, BLOCKS, LANES), BF),
        ),
        in_specs=[SMEM, SMEM] + [VMEM] * 6,
        out_specs=(VMEM, VMEM),
        scratch_shapes=[pltpu.VMEM((tok, D), F32), pltpu.VMEM((tok, BLOCKS, LANES), F32)],
        compiler_params=params(24),
        cost_estimate=cost(1 << 20, 5 << 20),
    )(pos, target, *parts, stream, gain)


def expert_kernel(scale, rows, gate, up, down, out, x, wg, wu, wd, gates, ups, act, part, done, in_sem, down_sem, out_sem):
    depth, hidden = wg.shape
    groups = OUT // LANES
    loads, downs, stores = [], [], []
    for i, j in enumerate(range(0, depth, DEEP)):
        at = pl.ds(j, DEEP)
        for k, (source, into) in enumerate(((rows, x), (gate, wg), (up, wu))):
            view = (source.at[:, at], into.at[:, at]) if k == 0 else (source.at[at], into.at[at])
            loads.append(pltpu.make_async_copy(*view, in_sem.at[3 * i + k]))
            loads[-1].start()
    for i, j in enumerate(range(0, depth, OUT)):
        at = pl.ds(j, OUT)
        downs.append(pltpu.make_async_copy(down.at[:, at], wd.at[:, at], down_sem.at[i]))
        downs[-1].start()
    for i, j in enumerate(range(0, depth, DEEP)):
        for load in loads[3 * i : 3 * i + 3]:
            load.wait()
        cut = x[:, j : j + DEEP]
        gate_part = jnp.dot(cut, wg[j : j + DEEP], preferred_element_type=F32)
        up_part = jnp.dot(cut, wu[j : j + DEEP], preferred_element_type=F32)
        if i == 0:
            gates[...] = gate_part
            ups[...] = up_part
        else:
            gates[...] += gate_part
            ups[...] += up_part
    gate_part = gates[...] * scale[0, 0]
    act[...] = (gate_part / (1.0 + jnp.exp(-gate_part)) * (ups[...] * scale[0, 1])).astype(BF)
    for load in downs:
        load.wait()
    for i, j in enumerate(range(0, depth, OUT)):
        total = jnp.dot(act[...], wd[:, j : j + OUT], preferred_element_type=F32) * scale[0, 2]
        two, first = i // 2, i % 2 * groups
        for g in range(groups):
            part[two % 2, :, first + g, :] = total[:, g * LANES : (g + 1) * LANES]
        if first:
            at = pl.ds(two * 2 * groups, 2 * groups)
            done[:, at, :] = part[two % 2].astype(BF)
            stores.append(pltpu.make_async_copy(done.at[:, at, :], out.at[:, at, :], out_sem.at[two]))
            stores[-1].start()
    for store in stores:
        store.wait()


def run_expert(scale, rows, gate, up, down):
    count, depth = rows.shape
    hidden = gate.shape[1]
    anywhere = pl.BlockSpec(memory_space=pl.ANY)
    return pl.pallas_call(
        expert_kernel,
        out_shape=jax.ShapeDtypeStruct((count, BLOCKS, LANES), BF),
        in_specs=[SMEM] + [anywhere] * 4,
        out_specs=anywhere,
        scratch_shapes=[
            pltpu.VMEM((count, depth), BF),
            pltpu.VMEM((depth, hidden), BF),
            pltpu.VMEM((depth, hidden), BF),
            pltpu.VMEM((hidden, depth), BF),
            pltpu.VMEM((count, hidden), F32),
            pltpu.VMEM((count, hidden), F32),
            pltpu.VMEM((count, hidden), BF),
            pltpu.VMEM((2, count, 2 * OUT // LANES, LANES), F32),
            pltpu.VMEM((count, BLOCKS, LANES), BF),
            pltpu.SemaphoreType.DMA((3 * depth // DEEP,)),
            pltpu.SemaphoreType.DMA((depth // OUT,)),
            pltpu.SemaphoreType.DMA((depth // (2 * OUT),)),
        ],
        compiler_params=params(56),
        cost_estimate=cost(6 * count * depth * hidden, 6 * depth * hidden),
    )(scale, rows, gate, up, down)


def mix_kernel(target, gates, results, res, out, mixed):
    tok = res.shape[0]

    def one_token(t, carry):
        add = gates[t, 0] * results[target[t, 0]].astype(F32)
        for k in range(1, TOPK):
            add += gates[t, k] * results[target[t, k]].astype(F32)
        mixed[t] = add
        return carry

    lax.fori_loop(0, tok, one_token, 0)
    for block in range(BLOCKS):
        lanes = slice(block * LANES, (block + 1) * LANES)
        out[:, lanes] = (res[:, lanes].astype(F32) + mixed[:, block, :]).astype(BF)


def mix(target, gates, results, res):
    tok = res.shape[0]
    return pl.pallas_call(
        mix_kernel,
        out_shape=jax.ShapeDtypeStruct((tok, D), BF),
        in_specs=[SMEM, SMEM, VMEM, VMEM],
        out_specs=VMEM,
        scratch_shapes=[pltpu.VMEM((tok, BLOCKS, LANES), F32)],
        compiler_params=params(16),
        cost_estimate=cost(1 << 20, 4 << 20),
    )(target, gates, results, res)


def body(
    query,
    key,
    value,
    head_gain,
    out_weight,
    stream,
    model_gain,
    expert_ids,
    expert_gates,
    gate_weight,
    up_weight,
    down_weight,
    weight_scales,
):
    seq = lax.axis_index("seq")
    head = lax.axis_index("head")
    x, y, z, c = seq // NY, seq % NY, head // NC, head % NC
    pos = jnp.stack([x, y, z, c]).astype(jnp.int32)
    seq_rows = query.shape[0]
    tok_rows = stream.shape[0]
    heads_local = head_gain.shape[0] // HD
    experts = lax.axis_size("seq") * lax.axis_size("head")
    slots = experts * CAP

    query_rows = query.reshape(seq_rows, heads_local, HD)
    key_rows = key.reshape(seq_rows, heads_local, HD)
    value_rows = value.reshape(seq_rows, heads_local, HD)
    block_state = jnp.einsum("shd,she->hde", key_rows, value_rows, preferred_element_type=F32)
    low = block_state.astype(BF)
    line, before = block_state, jnp.zeros_like(block_state)
    for d in range(1, NY):
        got = to_y(low, d).astype(F32)
        line = line + got
        before = before + jnp.where(y >= d, got, 0.0)
    low = line.astype(BF)
    totals = [to_x(low, d) for d in range(1, NX)]
    weights = [out_weight] + [to_y(out_weight, NY - d) for d in range(1, NY)]

    scores = jnp.einsum("thd,shd->hts", query_rows, key_rows, preferred_element_type=F32)
    causal = jnp.tril(jnp.ones((seq_rows, seq_rows), dtype=bool))
    scores = jnp.where(causal[None, :, :], scores, 0.0).astype(BF)
    local_part = jnp.einsum("hts,shd->thd", scores, value_rows, preferred_element_type=F32)
    local_part = local_part.reshape(seq_rows, heads_local * HD)
    head_normed = mixed_heads(pos, query, before, totals, local_part, head_gain[None])

    flat_ids = expert_ids.reshape(-1)
    at = jnp.arange(flat_ids.shape[0], dtype=jnp.int32)
    same = (flat_ids[:, None] == flat_ids[None, :]) & (at[None, :] < at[:, None])
    slot_index = jnp.sum(same.astype(jnp.int32), axis=1)
    target = (flat_ids * CAP + slot_index).reshape(tok_rows, TOPK)

    def exchange(rows):
        message = rows.reshape(experts, CAP * BLOCKS, LANES)
        got = lax.all_to_all(message, ("seq", "head"), split_axis=0, concat_axis=0, tiled=True)
        return got.reshape(slots, BLOCKS, LANES)

    tokens = [head_normed] + [to_x(head_normed, NX - d) for d in range(1, NX)]
    keep, give = project(pos, tokens, weights, tok_rows)
    own, *low = pair_sums(pos, keep, swap_core(give))
    sums = sum_z(own, [to_z(low[d - 1], d) for d in range(1, NZ)])
    parts = [sums[0]] + [to_x(sums[d], d) for d in range(1, NX)]
    res, message = place(pos, target, parts, stream, model_gain[None], slots)
    slot_rows = exchange(message).reshape(slots, D)
    produced = run_expert(weight_scales, slot_rows, gate_weight[0], up_weight[0], down_weight[0])
    results = exchange(produced)
    return mix(target, expert_gates, results, res)


def solution(mesh):
    token = P(("seq", "head"), None)
    expert = P(("seq", "head"), None, None)
    return jax.shard_map(
        body,
        mesh=mesh,
        in_specs=(
            P("seq", "head"),
            P("seq", "head"),
            P("seq", "head"),
            P("head"),
            P("head", "seq"),
            token,
            P(),
            token,
            token,
            expert,
            expert,
            expert,
            token,
        ),
        out_specs=token,
        check_vma=False,
    )
```

```python
import jax
import jax.numpy as jnp
from jax import lax
from jax.experimental import pallas as pl
from jax.experimental.pallas import tpu as pltpu
from jax.sharding import PartitionSpec as P

D = 4096
HD = 128
TOPK = 8
CAP = 3
NX, NY, NZ, NC = 4, 4, 4, 2
LANES = 128
BLOCKS = D // LANES
DEEP = 512
OUT = 1024
BF = jnp.bfloat16
F32 = jnp.float32


SMEM = pl.BlockSpec(memory_space=pltpu.SMEM)
VMEM = pl.BlockSpec(memory_space=pltpu.VMEM)


def params(mib):
    return pltpu.CompilerParams(vmem_limit_bytes=mib << 20)


def cost(flops, size):
    return pl.CostEstimate(flops=flops, bytes_accessed=size, transcendentals=0)


def to_x(a, d):
    pairs = [(x * NY + y, (x + d) % NX * NY + y) for x in range(NX) for y in range(NY)]
    return lax.ppermute(a, "seq", pairs)


def to_y(a, d):
    pairs = [(x * NY + y, x * NY + (y + d) % NY) for x in range(NX) for y in range(NY)]
    return lax.ppermute(a, "seq", pairs)


def to_z(a, d):
    pairs = [(z * NC + c, (z + d) % NZ * NC + c) for z in range(NZ) for c in range(NC)]
    return lax.ppermute(a, "head", pairs)


def swap_core(a):
    pairs = [(z * NC + c, z * NC + 1 - c) for z in range(NZ) for c in range(NC)]
    return lax.ppermute(a, "head", pairs)


def mixed_kernel(pos, query, before, one, two, three, local, gain, out):
    heads = before.shape[0]
    masks = [jnp.where(pos[0] >= d, 1.0, 0.0) for d in (1, 2, 3)]
    for h in range(heads):
        lanes = slice(h * HD, (h + 1) * HD)
        prior = before[h]
        for mask, got in zip(masks, (one, two, three)):
            prior += mask * got[h].astype(F32)
        mixed = local[:, lanes] + jnp.dot(query[:, lanes], prior.astype(BF), preferred_element_type=F32)
        mean_square = jnp.mean(mixed * mixed, axis=-1, keepdims=True)
        out[:, lanes] = (mixed * lax.rsqrt(mean_square + 1e-06) * gain[:, lanes]).astype(BF)


def mixed_heads(pos, query, before, totals, local, gain):
    return pl.pallas_call(
        mixed_kernel,
        out_shape=jax.ShapeDtypeStruct(query.shape, BF),
        in_specs=[SMEM] + [VMEM] * 7,
        out_specs=VMEM,
        compiler_params=params(16),
        cost_estimate=cost(1 << 25, 2 << 20),
    )(pos, query, before, *totals, local, gain)


def project_kernel(pos, *refs):
    blocks = len(refs) - NY - 3
    tokens, weights, (keep, give, rows) = refs[:blocks], refs[blocks : blocks + NY], refs[blocks + NY :]
    tok, wide = keep.shape[1], weights[0].shape[1]
    mine = pl.multiple_of(pos[3] * tok, tok)
    other = pl.multiple_of(tok - pos[3] * tok, tok)
    for dx in range(blocks):
        for dy in range(NY):
            rows[:, dy * wide : (dy + 1) * wide] = jnp.dot(
                tokens[dx][...], weights[dy][...], preferred_element_type=F32
            )
        for z in range(NZ):
            keep[dx * NZ + z] = rows[pl.ds(z * NC * tok + mine, tok), :]
            give[dx * NZ + z] = rows[pl.ds(z * NC * tok + other, tok), :].astype(BF)


def project(pos, tokens, weights, tok):
    wide = NY * weights[0].shape[1]
    shape = (len(tokens) * NZ, tok, wide)
    count, depth = tokens[0].shape
    return pl.pallas_call(
        project_kernel,
        out_shape=(jax.ShapeDtypeStruct(shape, F32), jax.ShapeDtypeStruct(shape, BF)),
        in_specs=[SMEM] + [VMEM] * (len(tokens) + NY),
        out_specs=(VMEM, VMEM),
        scratch_shapes=[pltpu.VMEM((count, wide), F32)],
        compiler_params=params(24),
        cost_estimate=cost(2 * len(tokens) * count * depth * wide, 5 << 20),
    )(pos, *tokens, *weights)


def pair_kernel(pos, keep, got, own, one, two, three):
    z = pos[2]
    for dx in range(own.shape[0]):
        at = dx * NZ + z
        own[dx] = keep[at] + got[at].astype(F32)
        for d, out in ((1, one), (2, two), (3, three)):
            at = dx * NZ + lax.rem(z + d, NZ)
            out[dx] = (keep[at] + got[at].astype(F32)).astype(BF)


def pair_sums(pos, keep, got):
    shape = (keep.shape[0] // NZ, *keep.shape[1:])
    low = jax.ShapeDtypeStruct(shape, BF)
    return pl.pallas_call(
        pair_kernel,
        out_shape=(jax.ShapeDtypeStruct(shape, F32), low, low, low),
        in_specs=[SMEM, VMEM, VMEM],
        out_specs=(VMEM,) * 4,
        compiler_params=params(16),
        cost_estimate=cost(1 << 20, 5 << 20),
    )(pos, keep, got)


def sum_kernel(own, one, two, three, *outs):
    for dx, out in enumerate(outs):
        total = own[dx] + one[dx].astype(F32) + two[dx].astype(F32) + three[dx].astype(F32)
        out[...] = total.astype(out.dtype)


def sum_z(own, parts, kinds):
    return pl.pallas_call(
        sum_kernel,
        out_shape=tuple(jax.ShapeDtypeStruct(own.shape[1:], kind) for kind in kinds),
        in_specs=[VMEM] * NZ,
        out_specs=(VMEM,) * len(kinds),
        compiler_params=params(16),
        cost_estimate=cost(1 << 20, 2 << 20),
    )(own, *parts)


def place_kernel(pos, target, own, one, two, three, stream, gain, res, message, total, scaled):
    tok = own.shape[0]
    wide = 2 * LANES
    x, y = pos[0], pos[1]
    squares = jnp.zeros((tok, LANES), F32)
    places = []
    for dx, part in enumerate((own, one, two, three)):
        for dy in range(NY):
            seq = lax.rem(x + NX - dx, NX) * NY + lax.rem(y + dy, NY)
            at = pl.multiple_of(seq * wide, wide)
            value = part[:, dy * wide : (dy + 1) * wide].astype(F32) + stream[:, pl.ds(at, wide)].astype(F32)
            value = value.astype(BF).astype(F32)
            j = dx * NY + dy
            total[:, j * wide : (j + 1) * wide] = value
            res[:, pl.ds(at, wide)] = value.astype(BF)
            for half in range(2):
                cut = value[:, half * LANES : (half + 1) * LANES]
                squares += cut * cut
            places.append((j, seq, at))
    factor = lax.rsqrt(jnp.sum(squares, axis=1, keepdims=True) * (1.0 / D) + 1e-06)
    for j, seq, at in places:
        value = total[:, j * wide : (j + 1) * wide] * factor * gain[:, pl.ds(at, wide)]
        for half in range(2):
            scaled[:, pl.ds(seq * 2 + half, 1), :] = value[:, half * LANES : (half + 1) * LANES][:, None, :]
    message[...] = jnp.zeros_like(message)

    def one_token(t, carry):
        row = scaled[t].astype(BF)
        for k in range(TOPK):
            message[target[t, k]] = row
        return carry

    lax.fori_loop(0, tok, one_token, 0)


def place(pos, target, parts, stream, gain, slots):
    tok = stream.shape[0]
    return pl.pallas_call(
        place_kernel,
        out_shape=(
            jax.ShapeDtypeStruct((tok, D), BF),
            jax.ShapeDtypeStruct((slots, BLOCKS, LANES), BF),
        ),
        in_specs=[SMEM, SMEM] + [VMEM] * 6,
        out_specs=(VMEM, VMEM),
        scratch_shapes=[pltpu.VMEM((tok, D), F32), pltpu.VMEM((tok, BLOCKS, LANES), F32)],
        compiler_params=params(24),
        cost_estimate=cost(1 << 20, 5 << 20),
    )(pos, target, *parts, stream, gain)


def expert_kernel(scale, rows, gate, up, down, out, x, wg, wu, wd, gates, ups, act, part, done, in_sem, down_sem, out_sem):
    depth, hidden = wg.shape
    groups = OUT // LANES
    loads, downs, stores = [], [], []
    for i, j in enumerate(range(0, depth, DEEP)):
        at = pl.ds(j, DEEP)
        for k, (source, into) in enumerate(((rows, x), (gate, wg), (up, wu))):
            view = (source.at[:, at], into.at[:, at]) if k == 0 else (source.at[at], into.at[at])
            loads.append(pltpu.make_async_copy(*view, in_sem.at[3 * i + k]))
            loads[-1].start()
    for i, j in enumerate(range(0, depth, OUT)):
        at = pl.ds(j, OUT)
        downs.append(pltpu.make_async_copy(down.at[:, at], wd.at[:, at], down_sem.at[i]))
        downs[-1].start()
    for i, j in enumerate(range(0, depth, DEEP)):
        for load in loads[3 * i : 3 * i + 3]:
            load.wait()
        cut = x[:, j : j + DEEP]
        gate_part = jnp.dot(cut, wg[j : j + DEEP], preferred_element_type=F32)
        up_part = jnp.dot(cut, wu[j : j + DEEP], preferred_element_type=F32)
        if i == 0:
            gates[...] = gate_part
            ups[...] = up_part
        else:
            gates[...] += gate_part
            ups[...] += up_part
    gate_part = gates[...] * scale[0, 0]
    act[...] = (gate_part / (1.0 + jnp.exp(-gate_part)) * (ups[...] * scale[0, 1])).astype(BF)
    for load in downs:
        load.wait()
    for i, j in enumerate(range(0, depth, OUT)):
        total = jnp.dot(act[...], wd[:, j : j + OUT], preferred_element_type=F32) * scale[0, 2]
        two, first = i // 2, i % 2 * groups
        for g in range(groups):
            part[two % 2, :, first + g, :] = total[:, g * LANES : (g + 1) * LANES]
        if first:
            at = pl.ds(two * 2 * groups, 2 * groups)
            done[:, at, :] = part[two % 2].astype(BF)
            stores.append(pltpu.make_async_copy(done.at[:, at, :], out.at[:, at, :], out_sem.at[two]))
            stores[-1].start()
    for store in stores:
        store.wait()


def run_expert(scale, rows, gate, up, down):
    count, depth = rows.shape
    hidden = gate.shape[1]
    anywhere = pl.BlockSpec(memory_space=pl.ANY)
    return pl.pallas_call(
        expert_kernel,
        out_shape=jax.ShapeDtypeStruct((count, BLOCKS, LANES), BF),
        in_specs=[SMEM] + [anywhere] * 4,
        out_specs=anywhere,
        scratch_shapes=[
            pltpu.VMEM((count, depth), BF),
            pltpu.VMEM((depth, hidden), BF),
            pltpu.VMEM((depth, hidden), BF),
            pltpu.VMEM((hidden, depth), BF),
            pltpu.VMEM((count, hidden), F32),
            pltpu.VMEM((count, hidden), F32),
            pltpu.VMEM((count, hidden), BF),
            pltpu.VMEM((2, count, 2 * OUT // LANES, LANES), F32),
            pltpu.VMEM((count, BLOCKS, LANES), BF),
            pltpu.SemaphoreType.DMA((3 * depth // DEEP,)),
            pltpu.SemaphoreType.DMA((depth // OUT,)),
            pltpu.SemaphoreType.DMA((depth // (2 * OUT),)),
        ],
        compiler_params=params(56),
        cost_estimate=cost(6 * count * depth * hidden, 6 * depth * hidden),
    )(scale, rows, gate, up, down)


def mix_kernel(target, gates, results, res, out, mixed):
    tok = res.shape[0]

    def one_token(t, carry):
        add = gates[t, 0] * results[target[t, 0]].astype(F32)
        for k in range(1, TOPK):
            add += gates[t, k] * results[target[t, k]].astype(F32)
        mixed[t] = add
        return carry

    lax.fori_loop(0, tok, one_token, 0)
    for block in range(BLOCKS):
        lanes = slice(block * LANES, (block + 1) * LANES)
        out[:, lanes] = (res[:, lanes].astype(F32) + mixed[:, block, :]).astype(BF)


def mix(target, gates, results, res):
    tok = res.shape[0]
    return pl.pallas_call(
        mix_kernel,
        out_shape=jax.ShapeDtypeStruct((tok, D), BF),
        in_specs=[SMEM, SMEM, VMEM, VMEM],
        out_specs=VMEM,
        scratch_shapes=[pltpu.VMEM((tok, BLOCKS, LANES), F32)],
        compiler_params=params(16),
        cost_estimate=cost(1 << 20, 4 << 20),
    )(target, gates, results, res)


def body(
    query,
    key,
    value,
    head_gain,
    out_weight,
    stream,
    model_gain,
    expert_ids,
    expert_gates,
    gate_weight,
    up_weight,
    down_weight,
    weight_scales,
):
    seq = lax.axis_index("seq")
    head = lax.axis_index("head")
    x, y, z, c = seq // NY, seq % NY, head // NC, head % NC
    pos = jnp.stack([x, y, z, c]).astype(jnp.int32)
    seq_rows = query.shape[0]
    tok_rows = stream.shape[0]
    heads_local = head_gain.shape[0] // HD
    experts = lax.axis_size("seq") * lax.axis_size("head")
    slots = experts * CAP

    query_rows = query.reshape(seq_rows, heads_local, HD)
    key_rows = key.reshape(seq_rows, heads_local, HD)
    value_rows = value.reshape(seq_rows, heads_local, HD)
    block_state = jnp.einsum("shd,she->hde", key_rows, value_rows, preferred_element_type=F32)
    low = block_state.astype(BF)
    line, before = block_state, jnp.zeros_like(block_state)
    for d in range(1, NY):
        got = to_y(low, d).astype(F32)
        line = line + got
        before = before + jnp.where(y >= d, got, 0.0)
    low = line.astype(BF)
    totals = [to_x(low, d) for d in range(1, NX)]
    weights = [out_weight] + [to_y(out_weight, NY - d) for d in range(1, NY)]

    scores = jnp.einsum("thd,shd->hts", query_rows, key_rows, preferred_element_type=F32)
    causal = jnp.tril(jnp.ones((seq_rows, seq_rows), dtype=bool))
    scores = jnp.where(causal[None, :, :], scores, 0.0).astype(BF)
    local_part = jnp.einsum("hts,shd->thd", scores, value_rows, preferred_element_type=F32)
    local_part = local_part.reshape(seq_rows, heads_local * HD)
    head_normed = mixed_heads(pos, query, before, totals, local_part, head_gain[None])

    flat_ids = expert_ids.reshape(-1)
    at = jnp.arange(flat_ids.shape[0], dtype=jnp.int32)
    same = (flat_ids[:, None] == flat_ids[None, :]) & (at[None, :] < at[:, None])
    slot_index = jnp.sum(same.astype(jnp.int32), axis=1)
    target = (flat_ids * CAP + slot_index).reshape(tok_rows, TOPK)

    def exchange(rows):
        message = rows.reshape(experts, CAP * BLOCKS, LANES)
        got = lax.all_to_all(message, ("seq", "head"), split_axis=0, concat_axis=0, tiled=True)
        return got.reshape(slots, BLOCKS, LANES)

    tokens = [head_normed] + [to_x(head_normed, NX - d) for d in range(1, NX)]
    parts, later = [], tokens[2:]
    for group in range(2):
        keep, give = project(pos, later if group else tokens[:2], weights, tok_rows)
        own, *low = pair_sums(pos, keep, swap_core(give))
        along_z = [to_z(low[d - 1], d) for d in range(1, NZ)]
        if group == 0:
            along_z[:2], later = lax.optimization_barrier((along_z[:2], later))
        kinds = (BF, BF) if parts else (F32, BF)
        sums = sum_z(own, along_z, kinds)
        for block in sums:
            parts.append(to_x(block, len(parts)) if parts else block)
    res, message = place(pos, target, parts, stream, model_gain[None], slots)
    slot_rows = exchange(message).reshape(slots, D)
    produced = run_expert(weight_scales, slot_rows, gate_weight[0], up_weight[0], down_weight[0])
    results = exchange(produced)
    return mix(target, expert_gates, results, res)


def solution(mesh):
    token = P(("seq", "head"), None)
    expert = P(("seq", "head"), None, None)
    return jax.shard_map(
        body,
        mesh=mesh,
        in_specs=(
            P("seq", "head"),
            P("seq", "head"),
            P("seq", "head"),
            P("head"),
            P("head", "seq"),
            token,
            P(),
            token,
            token,
            expert,
            expert,
            expert,
            token,
        ),
        out_specs=token,
        check_vma=False,
    )
```

```python
import jax
import jax.numpy as jnp
from jax import lax
from jax.experimental import pallas as pl
from jax.experimental.pallas import tpu as pltpu
from jax.sharding import PartitionSpec as P

D = 4096
HD = 128
TOPK = 8
CAP = 3
NX, NY, NZ, NC = 4, 4, 4, 2
LANES = 128
BLOCKS = D // LANES
DEEP = 512
OUT = 1024
BF = jnp.bfloat16
F32 = jnp.float32


SMEM = pl.BlockSpec(memory_space=pltpu.SMEM)
VMEM = pl.BlockSpec(memory_space=pltpu.VMEM)


def params(mib):
    return pltpu.CompilerParams(vmem_limit_bytes=mib << 20)


def cost(flops, size):
    return pl.CostEstimate(flops=flops, bytes_accessed=size, transcendentals=0)


def to_x(a, d):
    pairs = [(x * NY + y, (x + d) % NX * NY + y) for x in range(NX) for y in range(NY)]
    return lax.ppermute(a, "seq", pairs)


def to_y(a, d):
    pairs = [(x * NY + y, x * NY + (y + d) % NY) for x in range(NX) for y in range(NY)]
    return lax.ppermute(a, "seq", pairs)


def to_z(a, d):
    pairs = [(z * NC + c, (z + d) % NZ * NC + c) for z in range(NZ) for c in range(NC)]
    return lax.ppermute(a, "head", pairs)


def swap_core(a):
    pairs = [(z * NC + c, z * NC + 1 - c) for z in range(NZ) for c in range(NC)]
    return lax.ppermute(a, "head", pairs)


def mixed_kernel(pos, query, before, one, two, three, local, gain, out):
    heads = before.shape[0]
    masks = [jnp.where(pos[0] >= d, 1.0, 0.0) for d in (1, 2, 3)]
    for h in range(heads):
        lanes = slice(h * HD, (h + 1) * HD)
        prior = before[h]
        for mask, got in zip(masks, (one, two, three)):
            prior += mask * got[h].astype(F32)
        mixed = local[:, lanes] + jnp.dot(query[:, lanes], prior.astype(BF), preferred_element_type=F32)
        mean_square = jnp.mean(mixed * mixed, axis=-1, keepdims=True)
        out[:, lanes] = (mixed * lax.rsqrt(mean_square + 1e-06) * gain[:, lanes]).astype(BF)


def mixed_heads(pos, query, before, totals, local, gain):
    return pl.pallas_call(
        mixed_kernel,
        out_shape=jax.ShapeDtypeStruct(query.shape, BF),
        in_specs=[SMEM] + [VMEM] * 7,
        out_specs=VMEM,
        compiler_params=params(16),
        cost_estimate=cost(1 << 25, 2 << 20),
    )(pos, query, before, *totals, local, gain)


def project_kernel(pos, *refs):
    blocks = len(refs) - NY - 3
    tokens, weights, (keep, give, rows) = refs[:blocks], refs[blocks : blocks + NY], refs[blocks + NY :]
    tok, wide = keep.shape[1], weights[0].shape[1]
    mine = pl.multiple_of(pos[3] * tok, tok)
    other = pl.multiple_of(tok - pos[3] * tok, tok)
    for dx in range(blocks):
        for dy in range(NY):
            rows[:, dy * wide : (dy + 1) * wide] = jnp.dot(
                tokens[dx][...], weights[dy][...], preferred_element_type=F32
            )
        for z in range(NZ):
            keep[dx * NZ + z] = rows[pl.ds(z * NC * tok + mine, tok), :]
            give[dx * NZ + z] = rows[pl.ds(z * NC * tok + other, tok), :].astype(BF)


def project(pos, tokens, weights, tok):
    wide = NY * weights[0].shape[1]
    shape = (len(tokens) * NZ, tok, wide)
    count, depth = tokens[0].shape
    return pl.pallas_call(
        project_kernel,
        out_shape=(jax.ShapeDtypeStruct(shape, F32), jax.ShapeDtypeStruct(shape, BF)),
        in_specs=[SMEM] + [VMEM] * (len(tokens) + NY),
        out_specs=(VMEM, VMEM),
        scratch_shapes=[pltpu.VMEM((count, wide), F32)],
        compiler_params=params(24),
        cost_estimate=cost(2 * len(tokens) * count * depth * wide, 5 << 20),
    )(pos, *tokens, *weights)


def pair_kernel(pos, keep, got, own, one, two, three):
    z = pos[2]
    for dx in range(own.shape[0]):
        at = dx * NZ + z
        own[dx] = keep[at] + got[at].astype(F32)
        for d, out in ((1, one), (2, two), (3, three)):
            at = dx * NZ + lax.rem(z + d, NZ)
            out[dx] = (keep[at] + got[at].astype(F32)).astype(BF)


def pair_sums(pos, keep, got):
    shape = (keep.shape[0] // NZ, *keep.shape[1:])
    low = jax.ShapeDtypeStruct(shape, BF)
    return pl.pallas_call(
        pair_kernel,
        out_shape=(jax.ShapeDtypeStruct(shape, F32), low, low, low),
        in_specs=[SMEM, VMEM, VMEM],
        out_specs=(VMEM,) * 4,
        compiler_params=params(16),
        cost_estimate=cost(1 << 20, 5 << 20),
    )(pos, keep, got)


def sum_kernel(own, one, two, three, *outs):
    for dx, out in enumerate(outs):
        total = own[dx] + one[dx].astype(F32) + two[dx].astype(F32) + three[dx].astype(F32)
        out[...] = total.astype(out.dtype)


def sum_z(own, parts, kinds):
    return pl.pallas_call(
        sum_kernel,
        out_shape=tuple(jax.ShapeDtypeStruct(own.shape[1:], kind) for kind in kinds),
        in_specs=[VMEM] * NZ,
        out_specs=(VMEM,) * len(kinds),
        compiler_params=params(16),
        cost_estimate=cost(1 << 20, 2 << 20),
    )(own, *parts)


def place_kernel(pos, target, own, one, two, three, stream, gain, res, message, total, scaled):
    tok = own.shape[0]
    wide = 2 * LANES
    x, y = pos[0], pos[1]
    squares = jnp.zeros((tok, LANES), F32)
    places = []
    for dx, part in enumerate((own, one, two, three)):
        for dy in range(NY):
            seq = lax.rem(x + NX - dx, NX) * NY + lax.rem(y + dy, NY)
            at = pl.multiple_of(seq * wide, wide)
            value = part[:, dy * wide : (dy + 1) * wide].astype(F32) + stream[:, pl.ds(at, wide)].astype(F32)
            value = value.astype(BF).astype(F32)
            j = dx * NY + dy
            total[:, j * wide : (j + 1) * wide] = value
            res[:, pl.ds(at, wide)] = value.astype(BF)
            for half in range(2):
                cut = value[:, half * LANES : (half + 1) * LANES]
                squares += cut * cut
            places.append((j, seq, at))
    factor = lax.rsqrt(jnp.sum(squares, axis=1, keepdims=True) * (1.0 / D) + 1e-06)
    for j, seq, at in places:
        value = total[:, j * wide : (j + 1) * wide] * factor * gain[:, pl.ds(at, wide)]
        for half in range(2):
            scaled[:, pl.ds(seq * 2 + half, 1), :] = value[:, half * LANES : (half + 1) * LANES][:, None, :]
    message[...] = jnp.zeros_like(message)

    def one_token(t, carry):
        row = scaled[t].astype(BF)
        for k in range(TOPK):
            message[target[t, k]] = row
        return carry

    lax.fori_loop(0, tok, one_token, 0)


def place(pos, target, parts, stream, gain, slots):
    tok = stream.shape[0]
    return pl.pallas_call(
        place_kernel,
        out_shape=(
            jax.ShapeDtypeStruct((tok, D), BF),
            jax.ShapeDtypeStruct((slots, BLOCKS, LANES), BF),
        ),
        in_specs=[SMEM, SMEM] + [VMEM] * 6,
        out_specs=(VMEM, VMEM),
        scratch_shapes=[pltpu.VMEM((tok, D), F32), pltpu.VMEM((tok, BLOCKS, LANES), F32)],
        compiler_params=params(24),
        cost_estimate=cost(1 << 20, 5 << 20),
    )(pos, target, *parts, stream, gain)


def expert_kernel(scale, rows, gate, up, down, out, x, wg, wu, wd, gates, ups, act, part, done, in_sem, down_sem, out_sem):
    depth, hidden = wg.shape
    groups = OUT // LANES
    loads, downs, stores = [], [], []
    for i, j in enumerate(range(0, depth, DEEP)):
        at = pl.ds(j, DEEP)
        for k, (source, into) in enumerate(((rows, x), (gate, wg), (up, wu))):
            view = (source.at[:, at], into.at[:, at]) if k == 0 else (source.at[at], into.at[at])
            loads.append(pltpu.make_async_copy(*view, in_sem.at[3 * i + k]))
            loads[-1].start()
    for i, j in enumerate(range(0, depth, OUT)):
        at = pl.ds(j, OUT)
        downs.append(pltpu.make_async_copy(down.at[:, at], wd.at[:, at], down_sem.at[i]))
        downs[-1].start()
    for i, j in enumerate(range(0, depth, DEEP)):
        for load in loads[3 * i : 3 * i + 3]:
            load.wait()
        cut = x[:, j : j + DEEP]
        gate_part = jnp.dot(cut, wg[j : j + DEEP], preferred_element_type=F32)
        up_part = jnp.dot(cut, wu[j : j + DEEP], preferred_element_type=F32)
        if i == 0:
            gates[...] = gate_part
            ups[...] = up_part
        else:
            gates[...] += gate_part
            ups[...] += up_part
    gate_part = gates[...] * scale[0, 0]
    act[...] = (gate_part / (1.0 + jnp.exp(-gate_part)) * (ups[...] * scale[0, 1])).astype(BF)
    for load in downs:
        load.wait()
    for i, j in enumerate(range(0, depth, OUT)):
        total = jnp.dot(act[...], wd[:, j : j + OUT], preferred_element_type=F32) * scale[0, 2]
        two, first = i // 2, i % 2 * groups
        for g in range(groups):
            part[two % 2, :, first + g, :] = total[:, g * LANES : (g + 1) * LANES]
        if first:
            at = pl.ds(two * 2 * groups, 2 * groups)
            done[:, at, :] = part[two % 2].astype(BF)
            stores.append(pltpu.make_async_copy(done.at[:, at, :], out.at[:, at, :], out_sem.at[two]))
            stores[-1].start()
    for store in stores:
        store.wait()


def run_expert(scale, rows, gate, up, down):
    count, depth = rows.shape
    hidden = gate.shape[1]
    anywhere = pl.BlockSpec(memory_space=pl.ANY)
    return pl.pallas_call(
        expert_kernel,
        out_shape=jax.ShapeDtypeStruct((count, BLOCKS, LANES), BF),
        in_specs=[SMEM] + [anywhere] * 4,
        out_specs=anywhere,
        scratch_shapes=[
            pltpu.VMEM((count, depth), BF),
            pltpu.VMEM((depth, hidden), BF),
            pltpu.VMEM((depth, hidden), BF),
            pltpu.VMEM((hidden, depth), BF),
            pltpu.VMEM((count, hidden), F32),
            pltpu.VMEM((count, hidden), F32),
            pltpu.VMEM((count, hidden), BF),
            pltpu.VMEM((2, count, 2 * OUT // LANES, LANES), F32),
            pltpu.VMEM((count, BLOCKS, LANES), BF),
            pltpu.SemaphoreType.DMA((3 * depth // DEEP,)),
            pltpu.SemaphoreType.DMA((depth // OUT,)),
            pltpu.SemaphoreType.DMA((depth // (2 * OUT),)),
        ],
        compiler_params=params(56),
        cost_estimate=cost(6 * count * depth * hidden, 6 * depth * hidden),
    )(scale, rows, gate, up, down)


def mix_kernel(target, gates, results, res, out, mixed):
    tok = res.shape[0]

    def one_token(t, carry):
        add = gates[t, 0] * results[target[t, 0]].astype(F32)
        for k in range(1, TOPK):
            add += gates[t, k] * results[target[t, k]].astype(F32)
        mixed[t] = add
        return carry

    lax.fori_loop(0, tok, one_token, 0)
    for block in range(BLOCKS):
        lanes = slice(block * LANES, (block + 1) * LANES)
        out[:, lanes] = (res[:, lanes].astype(F32) + mixed[:, block, :]).astype(BF)


def mix(target, gates, results, res):
    tok = res.shape[0]
    return pl.pallas_call(
        mix_kernel,
        out_shape=jax.ShapeDtypeStruct((tok, D), BF),
        in_specs=[SMEM, SMEM, VMEM, VMEM],
        out_specs=VMEM,
        scratch_shapes=[pltpu.VMEM((tok, BLOCKS, LANES), F32)],
        compiler_params=params(16),
        cost_estimate=cost(1 << 20, 4 << 20),
    )(target, gates, results, res)


def body(
    query,
    key,
    value,
    head_gain,
    out_weight,
    stream,
    model_gain,
    expert_ids,
    expert_gates,
    gate_weight,
    up_weight,
    down_weight,
    weight_scales,
):
    seq = lax.axis_index("seq")
    head = lax.axis_index("head")
    x, y, z, c = seq // NY, seq % NY, head // NC, head % NC
    pos = jnp.stack([x, y, z, c]).astype(jnp.int32)
    seq_rows = query.shape[0]
    tok_rows = stream.shape[0]
    heads_local = head_gain.shape[0] // HD
    experts = lax.axis_size("seq") * lax.axis_size("head")
    slots = experts * CAP

    query_rows = query.reshape(seq_rows, heads_local, HD)
    key_rows = key.reshape(seq_rows, heads_local, HD)
    value_rows = value.reshape(seq_rows, heads_local, HD)
    block_state = jnp.einsum("shd,she->hde", key_rows, value_rows, preferred_element_type=F32)
    low = block_state.astype(BF)
    line, before = block_state, jnp.zeros_like(block_state)
    for d in range(1, NY):
        got = to_y(low, d).astype(F32)
        line = line + got
        before = before + jnp.where(y >= d, got, 0.0)
    low = line.astype(BF)
    totals = [to_x(low, d) for d in range(1, NX)]
    weights = [out_weight] + [to_y(out_weight, NY - d) for d in range(1, NY)]

    scores = jnp.einsum("thd,shd->hts", query_rows, key_rows, preferred_element_type=F32)
    causal = jnp.tril(jnp.ones((seq_rows, seq_rows), dtype=bool))
    scores = jnp.where(causal[None, :, :], scores, 0.0).astype(BF)
    local_part = jnp.einsum("hts,shd->thd", scores, value_rows, preferred_element_type=F32)
    local_part = local_part.reshape(seq_rows, heads_local * HD)
    head_normed = mixed_heads(pos, query, before, totals, local_part, head_gain[None])

    flat_ids = expert_ids.reshape(-1)
    at = jnp.arange(flat_ids.shape[0], dtype=jnp.int32)
    same = (flat_ids[:, None] == flat_ids[None, :]) & (at[None, :] < at[:, None])
    slot_index = jnp.sum(same.astype(jnp.int32), axis=1)
    target = (flat_ids * CAP + slot_index).reshape(tok_rows, TOPK)

    def exchange(rows):
        message = rows.reshape(experts, CAP * BLOCKS, LANES)
        got = lax.all_to_all(message, ("seq", "head"), split_axis=0, concat_axis=0, tiled=True)
        return got.reshape(slots, BLOCKS, LANES)

    tokens = [head_normed] + [to_x(head_normed, NX - d) for d in range(1, NX)]
    parts = []
    for group in (tokens[:2], tokens[2:]):
        keep, give = project(pos, group, weights, tok_rows)
        own, *low = pair_sums(pos, keep, swap_core(give))
        kinds = (BF, BF) if parts else (F32, BF)
        sums = sum_z(own, [to_z(low[d - 1], d) for d in range(1, NZ)], kinds)
        for block in sums:
            parts.append(to_x(block, len(parts)) if parts else block)
    res, message = place(pos, target, parts, stream, model_gain[None], slots)
    slot_rows = exchange(message).reshape(slots, D)
    produced = run_expert(weight_scales, slot_rows, gate_weight[0], up_weight[0], down_weight[0])
    results = exchange(produced)
    return mix(target, expert_gates, results, res)


def solution(mesh):
    token = P(("seq", "head"), None)
    expert = P(("seq", "head"), None, None)
    return jax.shard_map(
        body,
        mesh=mesh,
        in_specs=(
            P("seq", "head"),
            P("seq", "head"),
            P("seq", "head"),
            P("head"),
            P("head", "seq"),
            token,
            P(),
            token,
            token,
            expert,
            expert,
            expert,
            token,
        ),
        out_specs=token,
        check_vma=False,
    )
```
